256 devices in a mesh: seq: 64 (over z_hi, y, x), panel: 4 (over z_lo, core).
Axes of the slice: x: 4, y: 4, z: 8 (z_hi: 4, z_lo: 2; z = z_hi * 2 + z_lo), core: 2. Of those that a mesh axis runs over, the one named last changes fastest.
Arguments:
- tokens: bfloat16 [16384, 1024], P('seq', 'panel'), may hold values from -6 to 6
- cotangent: bfloat16 [16384, 1024], P('seq', 'panel'), may hold values from -6 to 6
- in_weight: bfloat16 [3, 1024, 1024], P(None, None, 'panel'), may hold values from -0.1875 to 0.1875
- short_kernel: float32 [3, 3, 1024], P(None, None, 'panel'), may hold values from -1 to 1
- skip_gain: float32 [1024], P('panel'), may hold values from 0.5 to 1.5
- long_filter: float32 [16384, 1024], P('seq', 'panel'), may hold values from -1.25 to 1.25
- out_weight: bfloat16 [1024, 1024], P('panel'), may hold values from -0.1875 to 0.1875
Outputs:
- block_out: bfloat16 [16384, 1024], P('seq', 'panel')
- token_grad: bfloat16 [16384, 1024], P('seq', 'panel')
The draws below stay inside these ranges and needn't reach their ends.
All inputs are finite; a program needn't handle non-finite values.
Results may differ from the reference program's by a relative error of at most 0.007.
Values may be sent and summed in bfloat16 or wider, within the bound.
A program may use at most 64 MiB of HBM per device.

```python
import math
import jax
import jax.numpy as jnp
from jax import lax

D = 1024
SHORT = 3
SEQ = 16384


def draw_long_filter(key, part):
    rate_key, noise_key, slow_key, tail_key = jax.random.split(jax.random.fold_in(key, 17), 4)
    rate_low, rate_high = (0.3, SEQ / 30.0)
    decay_rates = jnp.exp(jax.random.uniform(rate_key, (D,), jnp.float32, math.log(rate_low), math.log(rate_high)))
    position = jnp.arange(SEQ, dtype=jnp.float32)[:, None]
    envelope = jnp.exp(-decay_rates[None, :] * position / SEQ) * jnp.sqrt(2.0 * decay_rates / SEQ)[None, :]
    noise_part = jax.random.truncated_normal(noise_key, -4.0, 4.0, (SEQ, D), jnp.float32)
    slow_rates = jnp.exp(jax.random.uniform(slow_key, (D,), jnp.float32, math.log(0.2), math.log(1.0)))
    slow_norm = jnp.sqrt(2.0 * slow_rates / SEQ / (1.0 - jnp.exp(-2.0 * slow_rates)))
    slow_envelope = jnp.exp(-slow_rates[None, :] * position / SEQ) * slow_norm[None, :]
    tail_noise = jax.random.truncated_normal(tail_key, -4.0, 4.0, (SEQ, D), jnp.float32)
    return noise_part * envelope + 0.3 * tail_noise * slow_envelope


def block_levels(stream_key, shape, shards, least, top_value):
    def one(axis_at, shards_of):
        steps = jax.random.uniform(jax.random.fold_in(jax.random.fold_in(stream_key, 6), axis_at), (shards_of,), jnp.float32, least / len(shards), top_value / len(shards))
        return jnp.repeat(jnp.exp(steps), shape[axis_at] // shards_of).reshape((-1,) + (1,) * (len(shape) - axis_at - 1))

    loudness = one(*shards[0])
    for cut in shards[1:]:
        loudness = loudness * one(*cut)
    return loudness


def normal_values(stream_key, dims, scale, bound, shards=(), held_as=jnp.bfloat16):
    values = scale * jax.random.normal(stream_key, dims, jnp.float32)
    if shards:
        values = values * block_levels(stream_key, dims, shards, -0.22, 0.18)
    return jnp.clip(values, -bound, bound).astype(held_as)


def setup_inputs(seed: int = 0) -> dict:
    streams_of = jax.random.split(jax.random.key(seed), 8)
    return {
        "tokens": normal_values(streams_of[0], (SEQ, D), 1.0, 6.0, ((0, 64), (1, 4))),
        "cotangent": normal_values(streams_of[1], (SEQ, D), 1.0, 6.0, ((0, 64), (1, 4))),
        "in_weight": normal_values(streams_of[2], (3, D, D), D ** -0.5, 0.1875, ((2, 4),)),
        "short_kernel": jnp.clip(jax.random.uniform(streams_of[3], (SHORT, 3, D), jnp.float32, -1.0, 1.0) * block_levels(streams_of[3], (SHORT, 3, D), ((2, 4),), -0.4, 0.0), -1.0, 1.0),
        "skip_gain": jnp.clip(0.5 + 1.0 * jax.random.uniform(streams_of[4], (D,), jnp.float32) ** block_levels(streams_of[4], (D,), ((0, 4),), -0.2, 0.2), 0.5, 1.5),
        "long_filter": draw_long_filter(jax.random.fold_in(streams_of[7], 71), 0),
        "out_weight": normal_values(streams_of[6], (D, D), D ** -0.5, 0.1875, ((0, 4),)),
    }


def causal_short(projected, short_kernel):
    tap_count = short_kernel.shape[0]
    filtered = short_kernel[0][:, None, :] * projected
    for tap_index in range(1, tap_count):
        shifted = jnp.pad(projected[:, :-tap_index, :], ((0, 0), (tap_index, 0), (0, 0)))
        filtered = filtered + short_kernel[tap_index][:, None, :] * shifted
    return filtered


def anticausal_short(upstream, short_kernel):
    tap_count = short_kernel.shape[0]
    result = short_kernel[0][:, None, :] * upstream
    for tap_index in range(1, tap_count):
        shifted = jnp.pad(upstream[:, tap_index:, :], ((0, 0), (0, tap_index), (0, 0)))
        result = result + short_kernel[tap_index][:, None, :] * shifted
    return result


def long_conv(signal, long_filter, mirror):
    block_width = math.gcd(D, 128)
    groups = D // block_width
    sig_blocks = signal.reshape(SEQ, groups, block_width).transpose(1, 0, 2)
    fil_blocks = long_filter.reshape(SEQ, groups, block_width).transpose(1, 0, 2)

    def one_block(operands):
        sig_part, fil_part = operands
        sig_freq = jnp.fft.rfft(sig_part, n=2 * SEQ, axis=0)
        fil_freq = jnp.fft.rfft(fil_part, n=2 * SEQ, axis=0)
        if mirror:
            fil_freq = jnp.conj(fil_freq)
        return jnp.fft.irfft(sig_freq * fil_freq, n=2 * SEQ, axis=0)[:SEQ]

    result = lax.map(one_block, (sig_blocks, fil_blocks))
    return result.transpose(1, 0, 2).reshape(SEQ, D)


def reference(tokens, cotangent, in_weight, short_kernel, skip_gain, long_filter, out_weight):
    projected = jnp.stack([jnp.dot(tokens, in_weight[branch], preferred_element_type=jnp.float32) for branch in range(3)]).astype(jnp.bfloat16)
    filtered = causal_short(projected.astype(jnp.float32), short_kernel)
    gate_out, gate_in, value_path = filtered[0], filtered[1], filtered[2]
    signal = value_path * gate_in
    conv_state = long_conv(signal, long_filter, False) + skip_gain[None, :] * signal
    gated_state = (conv_state * gate_out).astype(jnp.bfloat16)
    block_out = jnp.dot(gated_state, out_weight, preferred_element_type=jnp.float32).astype(jnp.bfloat16)
    grad_gated = jnp.dot(cotangent, out_weight.T, preferred_element_type=jnp.float32)
    grad_gate_out = grad_gated * conv_state
    grad_state = grad_gated * gate_out
    grad_signal = long_conv(grad_state, long_filter, True) + skip_gain[None, :] * grad_state
    grad_value = grad_signal * gate_in
    grad_gate_in = grad_signal * value_path
    upstream = jnp.stack([grad_gate_out, grad_gate_in, grad_value])
    grad_projected = anticausal_short(upstream, short_kernel).astype(jnp.bfloat16)
    token_grad = jnp.dot(grad_projected[0], in_weight[0].T, preferred_element_type=jnp.float32)
    for branch in range(1, 3):
        token_grad = token_grad + jnp.dot(grad_projected[branch], in_weight[branch].T, preferred_element_type=jnp.float32)
    return block_out, token_grad.astype(jnp.bfloat16)
```

```python
import jax
import jax.numpy as jnp
from jax import lax
from jax.experimental import pallas as pl
from jax.experimental.pallas import tpu as pltpu
from jax.sharding import PartitionSpec as P

F32, BF16 = jnp.float32, jnp.bfloat16


def conv_kernel(x_ref, h_ref, y_ref, r_ref):
    row = lax.broadcasted_iota(jnp.int32, (128, 128), 0)
    col = lax.broadcasted_iota(jnp.int32, (128, 128), 1)
    keep = col >= row
    r_ref[128:256, 0:128] = jnp.zeros((128, 128), BF16)

    def build(k, prev):
        u = jnp.broadcast_to(h_ref[0, pl.ds(k, 1), :], (128, 128))
        v = pltpu.roll(u, 0, 1, stride=1, stride_axis=0)
        m = jnp.where(keep, v, prev).astype(BF16)
        at = pl.multiple_of(k * 128, 128)
        r_ref[0:128, pl.ds(at, 128)] = m
        r_ref[128:256, pl.ds(at + 128, 128)] = m
        return v

    lax.fori_loop(0, 128, build, jnp.zeros((128, 128), F32))

    sub = lax.broadcasted_iota(jnp.int32, (8, 2, 8, 256), 2)
    total = jnp.zeros((8, 2, 8, 256), F32)
    for r in range(8):
        z = jnp.dot(
            x_ref[0], r_ref[:, r * 256 : (r + 1) * 256], preferred_element_type=F32
        )
        for q in range(1, 8):
            at = (8 * q + r) * 256
            part = jnp.dot(
                x_ref[0, 0 : 128 - 16 * q, :],
                r_ref[:, at : at + 256],
                preferred_element_type=F32,
            )
            z = jnp.concatenate([z[: 16 * q], z[16 * q :] + part], axis=0)
        if r == 0:
            total = total + z.reshape(8, 2, 8, 256)
        else:
            turned = pltpu.roll(z.reshape(16, 8, 256), r, 1).reshape(8, 2, 8, 256)
            before = jnp.concatenate(
                [jnp.zeros((1, 2, 8, 256), F32), turned[:-1]], axis=0
            )
            total = total + jnp.where(sub >= r, turned, before)
    y_ref[0] = total.reshape(128, 256).astype(BF16)


def conv(x, h):
    return pl.pallas_call(
        conv_kernel,
        grid=(4,),
        out_shape=jax.ShapeDtypeStruct((4, 128, 256), BF16),
        in_specs=[
            pl.BlockSpec((1, 128, 256), lambda c: (c, 0, 0)),
            pl.BlockSpec((1, 128, 128), lambda c: (c, 0, 0)),
        ],
        out_specs=pl.BlockSpec((1, 128, 256), lambda c: (c, 0, 0)),
        scratch_shapes=[pltpu.VMEM((256, 16384 + 128), BF16)],
        compiler_params=pltpu.CompilerParams(vmem_limit_bytes=32 * 2**20),
    )(x, h)


def shifted(value, axis, steps):
    count = lax.axis_size(axis)
    initial, last = (max(0, -steps), min(count, count - steps))
    return lax.ppermute(value, axis, [(source, source + steps) for source in range(initial, last)])


def local(tokens, cotangent, in_weight, short_kernel, skip_gain, long_filter, out_weight):
    row_count = tokens.shape[0]
    tap_count = short_kernel.shape[0]
    n = lax.axis_size("seq")
    h = lax.all_to_all(
        long_filter.astype(BF16).T.reshape(n, 4, row_count), "seq", 0, 0
    )
    h = h.transpose(1, 0, 2).reshape(4, 128, 128).astype(F32)
    full_tok, full_cot = (
        lax.all_gather(tokens, "panel", axis=1, tiled=True),
        lax.all_gather(cotangent, "panel", axis=1, tiled=True),
    )
    projected = jnp.einsum(
        "td,jdc->jtc", full_tok, in_weight, preferred_element_type=F32
    ).astype(BF16)
    before = shifted(projected[:, row_count - (tap_count - 1) :, :], "seq", 1)
    extended = jnp.concatenate([before, projected], axis=1).astype(F32)
    filtered = short_kernel[0][:, None, :] * extended[:, tap_count - 1 :, :]
    for tap_index in range(1, tap_count):
        filtered = (
            filtered
            + short_kernel[tap_index][:, None, :]
            * extended[:, tap_count - 1 - tap_index : tap_count - 1 - tap_index + row_count, :]
        )
    gate_out, gate_in, value_path = (filtered[0], filtered[1], filtered[2])
    signal = value_path * gate_in
    grad_gated = lax.dot_general(
        full_cot, out_weight, (((1,), (1,)), ((), ())), preferred_element_type=F32
    )
    grad_state = grad_gated * gate_out

    both = jnp.stack([signal.T, grad_state[::-1].T], axis=1).astype(BF16)
    both = lax.all_to_all(both.reshape(n, 4, 2, row_count), "seq", 0, 0)
    xs = both[:, :, 0].transpose(1, 0, 2).reshape(4, 8, 1, 8, row_count)
    xg = both[::-1, :, 1].transpose(1, 0, 2).reshape(4, 8, 1, 8, row_count)
    x = jnp.concatenate([xs, xg], axis=2).reshape(4, 128, row_count)
    y = conv(x, h).reshape(4, 8, 2, 8, row_count)
    ys = y[:, :, 0].reshape(4, n, row_count).transpose(1, 0, 2)
    yg = y[:, :, 1].reshape(4, n, row_count).transpose(1, 0, 2)[::-1]
    back = lax.all_to_all(jnp.stack([ys, yg], axis=2), "seq", 0, 0).reshape(256, 2, row_count)
    conv_state = back[:, 0].T.astype(F32) + skip_gain[None, :] * signal
    grad_signal = back[:, 1].T[::-1].astype(F32) + skip_gain[None, :] * grad_state

    gated_state = (conv_state * gate_out).astype(BF16)
    partial_value = jnp.dot(gated_state, out_weight, preferred_element_type=F32)
    block_out = lax.psum_scatter(partial_value, "panel", scatter_dimension=1, tiled=True).astype(
        BF16
    )
    grad_gate_out = grad_gated * conv_state
    grad_value = grad_signal * gate_in
    grad_gate_in = grad_signal * value_path
    upstream = jnp.stack([grad_gate_out, grad_gate_in, grad_value])
    after_rim = shifted(upstream[:, : tap_count - 1, :], "seq", -1)
    widened = jnp.concatenate([upstream, after_rim], axis=1)
    grad_projected = short_kernel[0][:, None, :] * widened[:, :row_count, :]
    for tap_index in range(1, tap_count):
        grad_projected = (
            grad_projected
            + short_kernel[tap_index][:, None, :] * widened[:, tap_index : tap_index + row_count, :]
        )
    grad_projected = grad_projected.astype(BF16)
    grad_partial = jnp.einsum("jtc,jdc->td", grad_projected, in_weight, preferred_element_type=F32)
    token_grad = lax.psum_scatter(grad_partial, "panel", scatter_dimension=1, tiled=True).astype(
        BF16
    )
    return (block_out, token_grad)


def solution(mesh):
    placed = (
        P("seq", "panel"),
        P("seq", "panel"),
        P(None, None, "panel"),
        P(None, None, "panel"),
        P("panel"),
        P("seq", "panel"),
        P("panel", None),
    )
    return jax.shard_map(
        local,
        mesh=mesh,
        in_specs=placed,
        out_specs=(P("seq", "panel"), P("seq", "panel")),
        check_vma=False,
    )
```

```python
import functools

import jax
import jax.numpy as jnp
from jax import lax
from jax.experimental import pallas as pl
from jax.experimental.pallas import tpu as pltpu
from jax.sharding import PartitionSpec as P

F32, BF16 = jnp.float32, jnp.bfloat16


MESH = pl.DeviceIdType.MESH


def identity(flip):
    row = lax.broadcasted_iota(jnp.int32, (256, 256), 0)
    col = lax.broadcasted_iota(jnp.int32, (256, 256), 1)
    return jnp.where(row + col == 255 if flip else row == col, 1.0, 0.0).astype(BF16)


def turn(select, value):
    return lax.dot_general(select, value, (((1,), (1,)), ((), ())), preferred_element_type=F32)


def interleave(first, second):
    first, second = first.reshape(32, 8, 128), second.reshape(32, 8, 128)
    upper = lax.broadcasted_iota(jnp.int32, (32, 8, 128), 1) < 4
    even = jnp.where(upper, first, pltpu.roll(second, 4, 1))
    odd = jnp.where(upper, pltpu.roll(first, 4, 1), second)
    return even, odd


def exchange(n, send_ref, recv_ref, offset, sems):
    me = lax.axis_index("seq")

    def one(j, carry):
        to = lax.rem(me + j, n)
        pltpu.make_async_remote_copy(
            src_ref=send_ref.at[to],
            dst_ref=recv_ref.at[me + offset],
            send_sem=sems.at[0],
            recv_sem=sems.at[1],
            device_id={"seq": to},
            device_id_type=MESH,
        ).start()
        return carry

    lax.fori_loop(1, n, one, 0)
    recv_ref[me + offset] = send_ref[me]


def await_all(n, ref, sem):
    part = ref.at[pl.ds(0, n - 1)]
    pltpu.make_async_copy(part, part, sem).wait()


def build_toeplitz(hr, r_ref):
    row = lax.broadcasted_iota(jnp.int32, (128, 128), 0)
    col = lax.broadcasted_iota(jnp.int32, (128, 128), 1)
    cut = col >= 128 - row

    def channel(c, carry):
        r_ref[c, 128:256, 0:128] = jnp.zeros((128, 128), BF16)

        def block(a, carry):
            early = jnp.broadcast_to(hr[a, pl.ds(c + 4, 1), :], (128, 128))
            for half in range(2):
                now = jnp.broadcast_to(hr[a + 1, pl.ds(c + 4 * half, 1), :], (128, 128))
                mixed = jnp.where(cut, early, now)
                tile = pltpu.roll(mixed, 0, 1, stride=1, stride_axis=0).astype(BF16)
                at = pl.multiple_of(a * 256, 256) + 128 * half
                r_ref[c, 0:128, pl.ds(at, 128)] = tile
                r_ref[c, 128:256, pl.ds(at + 128, 128)] = tile
                early = now
            return carry

        lax.fori_loop(0, 64, block, 0, unroll=8)
        return carry

    lax.fori_loop(0, 4, channel, 0)


def convolve(xr, xf, xl, tot, r_ref, yf, ys):
    xf[...] = xr[...].astype(F32).reshape(1024, 128)
    for c in range(4):
        rows = []
        for j in range(8):
            s_at, g_at = 128 * j + c, 128 * (7 - j) + 4 + c
            for at in (s_at, g_at):
                rows.append(
                    jnp.concatenate(
                        [xf[pl.ds(at, 8, stride=16), :], xf[pl.ds(at + 8, 8, stride=16), :]], axis=1
                    )
                )
        x = jnp.concatenate(rows, axis=0).astype(BF16)
        xl[c, :, 0:256] = x
        for q in range(1, 8):
            xl[c, 0 : 16 * q, 256 * q : 256 * (q + 1)] = jnp.zeros((16 * q, 256), BF16)
            xl[c, 16 * q :, 256 * q : 256 * (q + 1)] = x[: 128 - 16 * q]

    sub = lax.broadcasted_iota(jnp.int32, (8, 8, 256), 1)

    def channel(c, carry):
        total = [None, None]
        for r in range(8):
            z = None
            for q in range(8):
                at = (8 * q + r) * 256
                part = jnp.dot(
                    xl[c, :, 256 * q : 256 * (q + 1)],
                    r_ref[c, :, at : at + 256],
                    preferred_element_type=F32,
                )
                z = part if z is None else z + part
            z = z.reshape(8, 2, 8, 256)
            for side in range(2):
                zs = z[:, side]
                if r == 0:
                    total[side] = zs
                    continue
                turned = pltpu.roll(zs, r if side == 0 else 8 - r, 1)
                before = jnp.concatenate([jnp.zeros((1, 8, 256), F32), turned[:-1]], axis=0)
                inside = sub >= r if side == 0 else sub < 8 - r
                total[side] = total[side] + jnp.where(inside, turned, before)
        for side in range(2):
            tot[c, side] = total[side]
        return carry

    lax.fori_loop(0, 4, channel, 0)
    for c in range(4):
        for j in range(8):
            s_at, g_at = 128 * j + c, 128 * (7 - j) + 4 + c
            for side, at in ((0, s_at), (1, g_at)):
                yf[pl.ds(at, 8, stride=16), :] = tot[c, side, j, :, 0:128]
                yf[pl.ds(at + 8, 8, stride=16), :] = tot[c, side, j, :, 128:256]
    ys[...] = yf[...].reshape(64, 16, 128).astype(BF16)


def conv_kernel(
    n, s_ref, g_ref, f_ref, so_ref, go_ref, hs, hr, xs, xr, xf, xl, tot, r_ref, yf, ys, yr, hsem, xsem, ysem
):
    me = lax.axis_index("seq")
    barrier = pltpu.get_barrier_semaphore()

    def greet(j, carry):
        pl.semaphore_signal(
            barrier, inc=1, device_id={"seq": lax.rem(me + j, n)}, device_id_type=MESH
        )
        return carry

    lax.fori_loop(1, n, greet, 0)
    eye, flip = identity(False), identity(True)
    ft = turn(eye, f_ref[...].astype(BF16))
    even, odd = interleave(ft[:, :128], ft[:, 128:])
    hs[...] = jnp.stack([even, odd], axis=1).reshape(64, 8, 128)
    hr[0] = jnp.zeros((8, 128), F32)
    pl.semaphore_wait(barrier, n - 1)
    exchange(n, hs, hr, 1, hsem)

    st = turn(eye, s_ref[...].astype(BF16))
    gf = jnp.dot(flip, g_ref[...].astype(BF16), preferred_element_type=F32)
    gt = turn(eye, gf.astype(BF16))
    even_lo, odd_lo = interleave(st[:, :128], gt[:, :128])
    even_hi, odd_hi = interleave(st[:, 128:], gt[:, 128:])
    even = jnp.concatenate([even_lo, even_hi], axis=1)
    odd = jnp.concatenate([odd_lo, odd_hi], axis=1)
    xs[...] = jnp.stack([even, odd], axis=1).reshape(64, 16, 128).astype(BF16)
    exchange(n, xs, xr, 0, xsem)

    await_all(n, hr, hsem.at[1])
    build_toeplitz(hr, r_ref)
    await_all(n, xr, xsem.at[1])
    convolve(xr, xf, xl, tot, r_ref, yf, ys)
    exchange(n, ys, yr, 0, ysem)
    await_all(n, yr, ysem.at[1])

    back = yr[...].astype(F32).reshape(32, 2, 16, 128)
    upper = lax.broadcasted_iota(jnp.int32, (32, 8, 128), 1) < 4
    cols_s, cols_g = [], []
    for half in range(2):
        even = back[:, 0, 8 * half : 8 * half + 8]
        odd = back[:, 1, 8 * half : 8 * half + 8]
        cols_s.append(jnp.where(upper, even, pltpu.roll(odd, 4, 1)).reshape(256, 128))
        cols_g.append(jnp.where(upper, pltpu.roll(even, 4, 1), odd).reshape(256, 128))
    so_ref[...] = turn(eye, jnp.concatenate(cols_s, axis=1).astype(BF16))
    go_ref[...] = turn(flip, jnp.concatenate(cols_g, axis=1).astype(BF16))
    await_all(n, hr, hsem.at[0])
    await_all(n, xr, xsem.at[0])
    await_all(n, yr, ysem.at[0])


def conv(signal, grad_state, long_filter):
    n = lax.axis_size("seq")
    out = jax.ShapeDtypeStruct((256, 256), F32)
    vmem = pl.BlockSpec(memory_space=pltpu.VMEM)
    return pl.pallas_call(
        functools.partial(conv_kernel, n),
        out_shape=(out, out),
        in_specs=[vmem] * 3,
        out_specs=(vmem, vmem),
        scratch_shapes=[
            pltpu.VMEM((64, 8, 128), F32),
            pltpu.VMEM((65, 8, 128), F32),
            pltpu.VMEM((64, 16, 128), BF16),
            pltpu.VMEM((64, 16, 128), BF16),
            pltpu.VMEM((1024, 128), F32),
            pltpu.VMEM((4, 128, 2048), BF16),
            pltpu.VMEM((4, 2, 8, 8, 256), F32),
            pltpu.VMEM((4, 256, 16384 + 128), BF16),
            pltpu.VMEM((1024, 128), F32),
            pltpu.VMEM((64, 16, 128), BF16),
            pltpu.VMEM((64, 16, 128), BF16),
            pltpu.SemaphoreType.DMA((2,)),
            pltpu.SemaphoreType.DMA((2,)),
            pltpu.SemaphoreType.DMA((2,)),
        ],
        compiler_params=pltpu.CompilerParams(
            collective_id=0, has_side_effects=True, vmem_limit_bytes=56 * 2**20
        ),
    )(signal, grad_state, long_filter)


def shifted(value, axis, steps):
    count = lax.axis_size(axis)
    initial, last = (max(0, -steps), min(count, count - steps))
    return lax.ppermute(value, axis, [(source, source + steps) for source in range(initial, last)])


def local(tokens, cotangent, in_weight, short_kernel, skip_gain, long_filter, out_weight):
    row_count = tokens.shape[0]
    tap_count = short_kernel.shape[0]
    full_tok, full_cot = (
        lax.all_gather(tokens, "panel", axis=1, tiled=True),
        lax.all_gather(cotangent, "panel", axis=1, tiled=True),
    )
    projected = jnp.einsum(
        "td,jdc->jtc", full_tok, in_weight, preferred_element_type=F32
    ).astype(BF16)
    before = shifted(projected[:, row_count - (tap_count - 1) :, :], "seq", 1)
    extended = jnp.concatenate([before, projected], axis=1).astype(F32)
    filtered = short_kernel[0][:, None, :] * extended[:, tap_count - 1 :, :]
    for tap_index in range(1, tap_count):
        filtered = (
            filtered
            + short_kernel[tap_index][:, None, :]
            * extended[:, tap_count - 1 - tap_index : tap_count - 1 - tap_index + row_count, :]
        )
    gate_out, gate_in, value_path = (filtered[0], filtered[1], filtered[2])
    signal = value_path * gate_in
    grad_gated = lax.dot_general(
        full_cot, out_weight, (((1,), (1,)), ((), ())), preferred_element_type=F32
    )
    grad_state = grad_gated * gate_out

    conv_out, grad_out = conv(signal, grad_state, long_filter)
    conv_state = conv_out + skip_gain[None, :] * signal
    grad_signal = grad_out + skip_gain[None, :] * grad_state

    gated_state = (conv_state * gate_out).astype(BF16)
    partial_value = jnp.dot(gated_state, out_weight, preferred_element_type=F32)
    block_out = lax.psum_scatter(partial_value, "panel", scatter_dimension=1, tiled=True).astype(
        BF16
    )
    grad_gate_out = grad_gated * conv_state
    grad_value = grad_signal * gate_in
    grad_gate_in = grad_signal * value_path
    upstream = jnp.stack([grad_gate_out, grad_gate_in, grad_value])
    after_rim = shifted(upstream[:, : tap_count - 1, :], "seq", -1)
    widened = jnp.concatenate([upstream, after_rim], axis=1)
    grad_projected = short_kernel[0][:, None, :] * widened[:, :row_count, :]
    for tap_index in range(1, tap_count):
        grad_projected = (
            grad_projected
            + short_kernel[tap_index][:, None, :] * widened[:, tap_index : tap_index + row_count, :]
        )
    grad_projected = grad_projected.astype(BF16)
    grad_partial = jnp.einsum("jtc,jdc->td", grad_projected, in_weight, preferred_element_type=F32)
    token_grad = lax.psum_scatter(grad_partial, "panel", scatter_dimension=1, tiled=True).astype(
        BF16
    )
    return (block_out, token_grad)


def solution(mesh):
    placed = (
        P("seq", "panel"),
        P("seq", "panel"),
        P(None, None, "panel"),
        P(None, None, "panel"),
        P("panel"),
        P("seq", "panel"),
        P("panel", None),
    )
    return jax.shard_map(
        local,
        mesh=mesh,
        in_specs=placed,
        out_specs=(P("seq", "panel"), P("seq", "panel")),
        check_vma=False,
    )
```

```python
import functools

import jax
import jax.numpy as jnp
from jax import lax
from jax.experimental import pallas as pl
from jax.experimental.pallas import tpu as pltpu
from jax.sharding import PartitionSpec as P

F32, BF16 = jnp.float32, jnp.bfloat16


MESH = pl.DeviceIdType.MESH


def identity(flip):
    row = lax.broadcasted_iota(jnp.int32, (256, 256), 0)
    col = lax.broadcasted_iota(jnp.int32, (256, 256), 1)
    return jnp.where(row + col == 255 if flip else row == col, 1.0, 0.0).astype(BF16)


def turn(select, value):
    return lax.dot_general(select, value, (((1,), (1,)), ((), ())), preferred_element_type=F32)


def interleave(first, second):
    first, second = first.reshape(32, 8, 128), second.reshape(32, 8, 128)
    upper = lax.broadcasted_iota(jnp.int32, (32, 8, 128), 1) < 4
    even = jnp.where(upper, first, pltpu.roll(second, 4, 1))
    odd = jnp.where(upper, pltpu.roll(first, 4, 1), second)
    return even, odd


def exchange(n, send_ref, recv_ref, offset, sems):
    me = lax.axis_index("seq")

    def one(j, carry):
        to = lax.rem(me + j, n)
        pltpu.make_async_remote_copy(
            src_ref=send_ref.at[to],
            dst_ref=recv_ref.at[me + offset],
            send_sem=sems.at[0],
            recv_sem=sems.at[1],
            device_id={"seq": to},
            device_id_type=MESH,
        ).start()
        return carry

    lax.fori_loop(1, n, one, 0)
    recv_ref[me + offset] = send_ref[me]


def await_all(n, ref, sem):
    part = ref.at[pl.ds(0, n - 1)]
    pltpu.make_async_copy(part, part, sem).wait()


def build_toeplitz(hr, r_ref):
    row = lax.broadcasted_iota(jnp.int32, (128, 128), 0)
    col = lax.broadcasted_iota(jnp.int32, (128, 128), 1)
    cut = col >= 128 - row

    def channel(c, carry):
        r_ref[c, 128:256, 0:128] = jnp.zeros((128, 128), BF16)

        def block(a, carry):
            early = jnp.broadcast_to(hr[a, pl.ds(c + 4, 1), :], (128, 128))
            for half in range(2):
                now = jnp.broadcast_to(hr[a + 1, pl.ds(c + 4 * half, 1), :], (128, 128))
                mixed = jnp.where(cut, early, now)
                tile = pltpu.roll(mixed, 0, 1, stride=1, stride_axis=0).astype(BF16)
                at = pl.multiple_of(a * 256, 256) + 128 * half
                r_ref[c, 0:128, pl.ds(at, 128)] = tile
                r_ref[c, 128:256, pl.ds(at + 128, 128)] = tile
                early = now
            return carry

        lax.fori_loop(0, 64, block, 0, unroll=8)
        return carry

    lax.fori_loop(0, 4, channel, 0)


def convolve(xr, xf, xl, tot, r_ref, yf, ys):
    xf[...] = xr[...].astype(F32).reshape(1024, 128)
    for c in range(4):
        rows = []
        for j in range(8):
            s_at, g_at = 128 * j + c, 128 * (7 - j) + 4 + c
            for at in (s_at, g_at):
                rows.append(
                    jnp.concatenate(
                        [xf[pl.ds(at, 8, stride=16), :], xf[pl.ds(at + 8, 8, stride=16), :]], axis=1
                    )
                )
        x = jnp.concatenate(rows, axis=0).astype(BF16)
        xl[c, :, 0:256] = x
        for q in range(1, 8):
            xl[c, 0 : 16 * q, 256 * q : 256 * (q + 1)] = jnp.zeros((16 * q, 256), BF16)
            xl[c, 16 * q :, 256 * q : 256 * (q + 1)] = x[: 128 - 16 * q]

    sub = lax.broadcasted_iota(jnp.int32, (8, 8, 256), 1)

    def channel(c, carry):
        total = [None, None]
        for r in range(8):
            z = None
            for q in range(8):
                at = (8 * q + r) * 256
                part = jnp.dot(
                    xl[c, :, 256 * q : 256 * (q + 1)],
                    r_ref[c, :, at : at + 256],
                    preferred_element_type=F32,
                )
                z = part if z is None else z + part
            z = z.reshape(8, 2, 8, 256)
            for side in range(2):
                zs = z[:, side]
                if r == 0:
                    total[side] = zs
                    continue
                turned = pltpu.roll(zs, r if side == 0 else 8 - r, 1)
                before = jnp.concatenate([jnp.zeros((1, 8, 256), F32), turned[:-1]], axis=0)
                inside = sub >= r if side == 0 else sub < 8 - r
                total[side] = total[side] + jnp.where(inside, turned, before)
        for side in range(2):
            tot[c, side] = total[side]
        return carry

    lax.fori_loop(0, 4, channel, 0)
    for c in range(4):
        for j in range(8):
            s_at, g_at = 128 * j + c, 128 * (7 - j) + 4 + c
            for side, at in ((0, s_at), (1, g_at)):
                yf[pl.ds(at, 8, stride=16), :] = tot[c, side, j, :, 0:128]
                yf[pl.ds(at + 8, 8, stride=16), :] = tot[c, side, j, :, 128:256]
    ys[...] = yf[...].reshape(64, 16, 128).astype(BF16)


def block_kernel(
    n, tok, cot, w_in_hbm, taps, skip, filt, w_out_hbm, out_ref, grad_ref,
    w_in, w_out, tokb, cotb, ext, gate, sig, gg, gs, hs, hr, xs, xr, xf, xl, tot, r_ref, yf, ys, yr,
    ups, edge, gp, own, half_send, half_recv, sum_send, sum_recv,
    wsem, tsem, fsem, esem, csem, hsem, xsem, ysem, usem, rsem, qsem,
):
    me, p = lax.axis_index("seq"), lax.axis_index("panel")
    core, chip = lax.rem(p, 2), p // 2
    sibling = chip * 2 + 1 - core
    across = (1 - chip) * 2 + core
    diagonal = (1 - chip) * 2 + 1 - core
    later, earlier = lax.rem(me + 1, n), lax.rem(me + n - 1, n)

    load_in = pltpu.make_async_copy(w_in_hbm, w_in, wsem.at[0])
    load_out = pltpu.make_async_copy(w_out_hbm, w_out, wsem.at[1])
    load_in.start()
    load_out.start()

    barrier = pltpu.get_barrier_semaphore()

    def signal(seq, panel):
        pl.semaphore_signal(
            barrier, inc=1, device_id={"seq": seq, "panel": panel}, device_id_type=MESH
        )

    signal(me, sibling)
    signal(me, across)
    for other in (sibling, across, diagonal):
        signal(earlier, other)

    def greet(j, carry):
        signal(lax.rem(me + j, n), p)
        return carry

    lax.fori_loop(1, n, greet, 0)

    def send(src, dst, sems, seq, panel):
        copy = pltpu.make_async_remote_copy(
            src_ref=src,
            dst_ref=dst,
            send_sem=sems.at[0],
            recv_sem=sems.at[1],
            device_id={"seq": seq, "panel": panel},
            device_id_type=MESH,
        )
        copy.start()
        return copy

    eye, flip = identity(False), identity(True)
    ft = turn(eye, filt[...].astype(BF16))
    even, odd = interleave(ft[:, :128], ft[:, 128:])
    hs[...] = jnp.stack([even, odd], axis=1).reshape(64, 8, 128)
    hr[0] = jnp.zeros((8, 128), F32)
    tokb[p, 16:272, :] = tok[...]
    cotb[p] = cot[...]
    pl.semaphore_wait(barrier, n + 4)

    body = pl.ds(16, 256)
    rim = pl.ds(0, 16)
    tok_across = send(tok, tokb.at[p, body], tsem.at[0], me, across)
    tok_sibling = send(tok, tokb.at[p, body], tsem.at[1], me, sibling)
    edges = [
        send(tok.at[pl.ds(240, 16)], tokb.at[p, rim], esem.at[slot], later, panel)
        for slot, panel in enumerate((p, sibling, across, diagonal))
    ]
    cot_across = send(cot, cotb.at[p], csem.at[0], me, across)
    cot_sibling = send(cot, cotb.at[p], csem.at[1], me, sibling)
    exchange(n, hs, hr, 1, hsem)
    tok_across.wait_recv()
    tok_forward = send(tokb.at[across, body], tokb.at[across, body], fsem.at[0], me, sibling)
    tok_sibling.wait_recv()
    for copy in edges:
        copy.wait_recv()
    tok_forward.wait_recv()
    load_in.wait()

    started = (me > 0).astype(F32)
    for j in range(3):
        value = None
        for k in range(4):
            part = jnp.dot(
                tokb[k], w_in[j, 256 * k : 256 * (k + 1), :], preferred_element_type=F32
            )
            value = part if value is None else value + part
        value = value.astype(BF16).astype(F32)
        ext[j, 0:16, :] = value[0:16] * started
        ext[j, 16:272, :] = value[16:]
    for j in range(3):
        gate[j] = (
            taps[0, j : j + 1, :] * ext[j, 16:272, :]
            + taps[1, j : j + 1, :] * ext[j, 15:271, :]
            + taps[2, j : j + 1, :] * ext[j, 14:270, :]
        )
    sig[...] = gate[2] * gate[1]
    st = turn(eye, sig[...].astype(BF16))

    cot_across.wait_recv()
    cot_forward = send(cotb.at[across], cotb.at[across], fsem.at[1], me, sibling)
    cot_sibling.wait_recv()
    cot_forward.wait_recv()
    load_out.wait()
    value = None
    for k in range(4):
        part = lax.dot_general(
            cotb[k],
            w_out[:, 256 * k : 256 * (k + 1)],
            (((1,), (1,)), ((), ())),
            preferred_element_type=F32,
        )
        value = part if value is None else value + part
    gg[...] = value
    gs[...] = value * gate[0]
    gf = jnp.dot(flip, gs[...].astype(BF16), preferred_element_type=F32)
    gt = turn(eye, gf.astype(BF16))
    even_lo, odd_lo = interleave(st[:, :128], gt[:, :128])
    even_hi, odd_hi = interleave(st[:, 128:], gt[:, 128:])
    even = jnp.concatenate([even_lo, even_hi], axis=1)
    odd = jnp.concatenate([odd_lo, odd_hi], axis=1)
    xs[...] = jnp.stack([even, odd], axis=1).reshape(64, 16, 128).astype(BF16)
    exchange(n, xs, xr, 0, xsem)

    await_all(n, hr, hsem.at[1])
    build_toeplitz(hr, r_ref)
    await_all(n, xr, xsem.at[1])
    convolve(xr, xf, xl, tot, r_ref, yf, ys)
    exchange(n, ys, yr, 0, ysem)
    await_all(n, yr, ysem.at[1])

    back = yr[...].astype(F32).reshape(32, 2, 16, 128)
    upper = lax.broadcasted_iota(jnp.int32, (32, 8, 128), 1) < 4
    cols_s, cols_g = [], []
    for half in range(2):
        even = back[:, 0, 8 * half : 8 * half + 8]
        odd = back[:, 1, 8 * half : 8 * half + 8]
        cols_s.append(jnp.where(upper, even, pltpu.roll(odd, 4, 1)).reshape(256, 128))
        cols_g.append(jnp.where(upper, pltpu.roll(even, 4, 1), odd).reshape(256, 128))
    state = turn(eye, jnp.concatenate(cols_s, axis=1).astype(BF16)) + skip[...] * sig[...]
    grad_signal = turn(flip, jnp.concatenate(cols_g, axis=1).astype(BF16)) + skip[...] * gs[...]
    ups[0, 0:256, :] = gg[...] * state
    ups[1, 0:256, :] = grad_signal * gate[2]
    ups[2, 0:256, :] = grad_signal * gate[1]
    rim_copy = send(ups.at[:, pl.ds(0, 8)], edge, usem, earlier, p)

    def scatter_sum(which, product):
        half_send[which, 0] = product(sibling).astype(BF16)
        half_send[which, 1] = product(diagonal).astype(BF16)
        first = send(half_send.at[which], half_recv.at[which], rsem.at[which], me, sibling)
        own[which] = product(p)
        value = product(across)
        first.wait_recv()
        sum_send[which] = (value + half_recv[which, 1].astype(F32)).astype(BF16)
        second = send(sum_send.at[which], sum_recv.at[which], qsem.at[which], me, across)
        own[which] = own[which] + half_recv[which, 0].astype(F32)
        return first, second

    gated = (state * gate[0]).astype(BF16)

    def out_product(k):
        cols = pl.ds(pl.multiple_of(k * 256, 256), 256)
        return jnp.dot(gated, w_out[:, cols], preferred_element_type=F32)

    sent = scatter_sum(0, out_product)

    rim_copy.wait_recv()
    ups[:, 256:264, :] = edge[...] * (me < n - 1).astype(F32)
    for j in range(3):
        gp[j] = (
            taps[0, j : j + 1, :] * ups[j, 0:256, :]
            + taps[1, j : j + 1, :] * ups[j, 1:257, :]
            + taps[2, j : j + 1, :] * ups[j, 2:258, :]
        ).astype(BF16)

    def grad_product(k):
        rows = pl.ds(pl.multiple_of(k * 256, 256), 256)
        value = None
        for j in range(3):
            part = lax.dot_general(
                gp[j], w_in[j, rows, :], (((1,), (1,)), ((), ())), preferred_element_type=F32
            )
            value = part if value is None else value + part
        return value

    sent = sent + scatter_sum(1, grad_product)
    sent[1].wait_recv()
    out_ref[...] = (own[0] + sum_recv[0].astype(F32)).astype(BF16)
    sent[3].wait_recv()
    grad_ref[...] = (own[1] + sum_recv[1].astype(F32)).astype(BF16)

    for copy in (tok_across, tok_sibling, tok_forward, cot_across, cot_sibling, cot_forward, rim_copy):
        copy.wait_send()
    for copy in tuple(edges) + sent:
        copy.wait_send()
    await_all(n, hr, hsem.at[0])
    await_all(n, xr, xsem.at[0])
    await_all(n, yr, ysem.at[0])


def local(tokens, cotangent, in_weight, short_kernel, skip_gain, long_filter, out_weight):
    n = lax.axis_size("seq")
    out = jax.ShapeDtypeStruct((256, 256), BF16)
    vmem = pl.BlockSpec(memory_space=pltpu.VMEM)
    hbm = pl.BlockSpec(memory_space=pl.ANY)
    sem = pltpu.SemaphoreType.DMA
    return pl.pallas_call(
        functools.partial(block_kernel, n),
        out_shape=(out, out),
        in_specs=[vmem, vmem, hbm, vmem, vmem, vmem, hbm],
        out_specs=(vmem, vmem),
        scratch_shapes=[
            pltpu.VMEM((3, 1024, 256), BF16),
            pltpu.VMEM((256, 1024), BF16),
            pltpu.VMEM((4, 272, 256), BF16),
            pltpu.VMEM((4, 256, 256), BF16),
            pltpu.VMEM((3, 272, 256), F32),
            pltpu.VMEM((3, 256, 256), F32),
            pltpu.VMEM((256, 256), F32),
            pltpu.VMEM((256, 256), F32),
            pltpu.VMEM((256, 256), F32),
            pltpu.VMEM((64, 8, 128), F32),
            pltpu.VMEM((65, 8, 128), F32),
            pltpu.VMEM((64, 16, 128), BF16),
            pltpu.VMEM((64, 16, 128), BF16),
            pltpu.VMEM((1024, 128), F32),
            pltpu.VMEM((4, 128, 2048), BF16),
            pltpu.VMEM((4, 2, 8, 8, 256), F32),
            pltpu.VMEM((4, 256, 16384 + 128), BF16),
            pltpu.VMEM((1024, 128), F32),
            pltpu.VMEM((64, 16, 128), BF16),
            pltpu.VMEM((64, 16, 128), BF16),
            pltpu.VMEM((3, 264, 256), F32),
            pltpu.VMEM((3, 8, 256), F32),
            pltpu.VMEM((3, 256, 256), BF16),
            pltpu.VMEM((2, 256, 256), F32),
            pltpu.VMEM((2, 2, 256, 256), BF16),
            pltpu.VMEM((2, 2, 256, 256), BF16),
            pltpu.VMEM((2, 256, 256), BF16),
            pltpu.VMEM((2, 256, 256), BF16),
            sem((2,)),
            sem((2, 2)),
            sem((2, 2)),
            sem((4, 2)),
            sem((2, 2)),
            sem((2,)),
            sem((2,)),
            sem((2,)),
            sem((2,)),
            sem((2, 2)),
            sem((2, 2)),
        ],
        compiler_params=pltpu.CompilerParams(
            collective_id=0, has_side_effects=True, vmem_limit_bytes=58 * 2**20
        ),
    )(
        tokens,
        cotangent,
        in_weight,
        short_kernel,
        skip_gain.reshape(1, -1),
        long_filter,
        out_weight,
    )


def solution(mesh):
    placed = (
        P("seq", "panel"),
        P("seq", "panel"),
        P(None, None, "panel"),
        P(None, None, "panel"),
        P("panel"),
        P("seq", "panel"),
        P("panel", None),
    )
    return jax.shard_map(
        local,
        mesh=mesh,
        in_specs=placed,
        out_specs=(P("seq", "panel"), P("seq", "panel")),
        check_vma=False,
    )
```

```python
import functools

import jax
import jax.numpy as jnp
from jax import lax
from jax.experimental import pallas as pl
from jax.experimental.pallas import tpu as pltpu
from jax.sharding import PartitionSpec as P

F32, BF16 = jnp.float32, jnp.bfloat16


MESH = pl.DeviceIdType.MESH


def identity(flip):
    row = lax.broadcasted_iota(jnp.int32, (256, 256), 0)
    col = lax.broadcasted_iota(jnp.int32, (256, 256), 1)
    return jnp.where(row + col == 255 if flip else row == col, 1.0, 0.0).astype(BF16)


def turn(select, value):
    return lax.dot_general(select, value, (((1,), (1,)), ((), ())), preferred_element_type=F32)


def spread():
    half = lax.broadcasted_iota(jnp.int32, (2, 512, 256), 0)
    row = lax.broadcasted_iota(jnp.int32, (2, 512, 256), 1)
    col = lax.broadcasted_iota(jnp.int32, (2, 512, 256), 2)
    return jnp.where(col + (col // 4) * 4 + 4 * half == row, 1.0, 0.0).astype(BF16)


def collect(pair):
    row = lax.broadcasted_iota(jnp.int32, (1024, 512), 0)
    col = lax.broadcasted_iota(jnp.int32, (1024, 512), 1)
    channel = row % 256
    source = (channel // 4) * 8 + 2 * (row // 256) + channel % 2
    return jnp.where((col == source) & ((channel // 2) % 2 == pair), 1.0, 0.0).astype(BF16)


def chunks(spread_ref, value):
    rows = turn(spread_ref[0], value[:128]) + turn(spread_ref[1], value[128:])
    return rows.reshape(64, 8, 128).astype(BF16)


def exchange(n, send_ref, recv_ref, offset, sems):
    me = lax.axis_index("seq")

    def one(j, carry):
        to = lax.rem(me + j, n)
        pltpu.make_async_remote_copy(
            src_ref=send_ref.at[to],
            dst_ref=recv_ref.at[me + offset],
            send_sem=sems.at[0],
            recv_sem=sems.at[1],
            device_id={"seq": to},
            device_id_type=MESH,
        ).start()
        return carry

    lax.fori_loop(1, n, one, 0, unroll=9)
    recv_ref[me + offset] = send_ref[me]


def await_all(n, ref, sem):
    part = ref.at[pl.ds(0, n - 1)]
    pltpu.make_async_copy(part, part, sem).wait()


def build_toeplitz(hc, r_ref, first, last):
    row = lax.broadcasted_iota(jnp.int32, (128, 128), 0)
    col = lax.broadcasted_iota(jnp.int32, (128, 128), 1)
    cut = col >= 128 - row

    def channel(c, carry):
        r_ref[c, 128:256, 0:128] = jnp.zeros((128, 128), BF16)
        early = jnp.zeros((128, 128), F32)
        for k in range(128):
            now = jnp.broadcast_to(hc[c, k : k + 1, :], (128, 128))
            mixed = jnp.where(cut, early, now)
            tile = pltpu.roll(mixed, 0, 1, stride=1, stride_axis=0).astype(BF16)
            at = 128 * k
            r_ref[c, 0:128, at : at + 128] = tile
            r_ref[c, 128:256, at + 128 : at + 256] = tile
            early = now
        return carry

    lax.fori_loop(first, last, channel, 0)


def shifted_blocks(sr, gr, sf, gf, xl):
    sf[...] = sr[...].astype(F32).reshape(512, 128)
    gf[...] = gr[...].astype(F32).reshape(512, 128)
    for c in range(4):
        rows = []
        for j in range(8):
            for ref, at in ((sf, 64 * j + c), (gf, 64 * (7 - j) + c)):
                rows.append(
                    jnp.concatenate(
                        [ref[pl.ds(at, 8, stride=8), :], ref[pl.ds(at + 4, 8, stride=8), :]], axis=1
                    )
                )
        x = jnp.concatenate(rows, axis=0).astype(BF16)
        xl[c, :, 0:256] = x
        for q in range(1, 8):
            xl[c, 0 : 16 * q, 256 * q : 256 * (q + 1)] = jnp.zeros((16 * q, 256), BF16)
            xl[c, 16 * q :, 256 * q : 256 * (q + 1)] = x[: 128 - 16 * q]


def convolve(pair, xl, r_ref, yf, ys):
    sub = lax.broadcasted_iota(jnp.int32, (8, 8, 256), 1)

    def channel(t, carry):
        c = 2 * pair + t
        total = [None, None]
        for r in range(8):
            z = None
            for q in range(8):
                at = (8 * q + r) * 256
                part = jnp.dot(
                    xl[c, :, 256 * q : 256 * (q + 1)],
                    r_ref[c, :, at : at + 256],
                    preferred_element_type=F32,
                )
                z = part if z is None else z + part
            z = z.reshape(8, 2, 8, 256)
            for side in range(2):
                zs = z[:, side]
                if r == 0:
                    total[side] = zs
                    continue
                turned = pltpu.roll(zs, r if side == 0 else 8 - r, 1)
                before = jnp.concatenate([jnp.zeros((1, 8, 256), F32), turned[:-1]], axis=0)
                inside = sub >= r if side == 0 else sub < 8 - r
                total[side] = total[side] + jnp.where(inside, turned, before)
        for side in range(2):
            for j in range(8):
                at = 64 * (j if side == 0 else 7 - j) + 2 * side
                yf[pl.ds(at + t, 8, stride=8), :] = total[side][j, :, 0:128]
                yf[pl.ds(at + 4 + t, 8, stride=8), :] = total[side][j, :, 128:256]
        return carry

    lax.fori_loop(0, 2, channel, 0)
    ys[pair] = yf[...].reshape(64, 8, 128).astype(BF16)


def block_kernel(
    n, tok, cot, w_in_hbm, taps, skip, filt, w_out_hbm, out_ref, grad_ref,
    w_in, w_out, tokb, cotb, ext, gate, sig, gg, gs, es, cs, hs, hr, hf, hc, ss, sr, sf, gx, gr, gf, xl, r_ref, yf, ys, yr,
    ups, edge, gp, own, half_send, half_recv, sum_send, sum_recv,
    wsem, tsem, fsem, esem, csem, hsem, ssem, gsem, ysem, usem, rsem, qsem,
):
    me, p = lax.axis_index("seq"), lax.axis_index("panel")
    core, chip = lax.rem(p, 2), p // 2
    sibling = chip * 2 + 1 - core
    across = (1 - chip) * 2 + core
    diagonal = (1 - chip) * 2 + 1 - core
    later, earlier = lax.rem(me + 1, n), lax.rem(me + n - 1, n)

    load_in = pltpu.make_async_copy(w_in_hbm, w_in, wsem.at[0])
    load_out = pltpu.make_async_copy(w_out_hbm, w_out, wsem.at[1])
    load_in.start()
    load_out.start()

    barrier = pltpu.get_barrier_semaphore()

    def signal(seq, panel):
        pl.semaphore_signal(
            barrier, inc=1, device_id={"seq": seq, "panel": panel}, device_id_type=MESH
        )

    signal(me, sibling)
    signal(me, across)
    for other in (sibling, across, diagonal):
        signal(earlier, other)

    def greet(j, carry):
        signal(lax.rem(me + j, n), p)
        return carry

    lax.fori_loop(1, n, greet, 0, unroll=9)

    def send(src, dst, sems, seq, panel):
        copy = pltpu.make_async_remote_copy(
            src_ref=src,
            dst_ref=dst,
            send_sem=sems.at[0],
            recv_sem=sems.at[1],
            device_id={"seq": seq, "panel": panel},
            device_id_type=MESH,
        )
        copy.start()
        return copy

    pl.semaphore_wait(barrier, n + 4)

    body = pl.ds(16, 256)
    rim = pl.ds(0, 16)
    tok_across = send(tok, tokb.at[p, body], tsem.at[0], me, across)
    tok_sibling = send(tok, tokb.at[p, body], tsem.at[1], me, sibling)
    edges = [
        send(tok.at[pl.ds(240, 16)], tokb.at[p, rim], esem.at[slot], later, panel)
        for slot, panel in enumerate((p, sibling, across, diagonal))
    ]
    es[...] = spread()
    hs[...] = chunks(es, filt[...].astype(BF16))
    hr[0] = jnp.zeros((8, 128), BF16)
    exchange(n, hs, hr, 1, hsem)
    cot_across = send(cot, cotb.at[p], csem.at[0], me, across)
    cot_sibling = send(cot, cotb.at[p], csem.at[1], me, sibling)
    tokb[p, 16:272, :] = tok[...]
    cotb[p] = cot[...]
    cs[0] = collect(0)
    cs[1] = collect(1)
    eye, flip = identity(False), identity(True)
    tok_across.wait_recv()
    tok_forward = send(tokb.at[across, body], tokb.at[across, body], fsem.at[0], me, sibling)
    tok_sibling.wait_recv()
    for copy in edges:
        copy.wait_recv()
    tok_forward.wait_recv()
    load_in.wait()

    started = (me > 0).astype(F32)
    for j in range(3):
        value = None
        for k in range(4):
            part = jnp.dot(
                tokb[k], w_in[j, 256 * k : 256 * (k + 1), :], preferred_element_type=F32
            )
            value = part if value is None else value + part
        value = value.astype(BF16).astype(F32)
        ext[j, 0:16, :] = value[0:16] * started
        ext[j, 16:272, :] = value[16:]
    for j in range(3):
        gate[j] = (
            taps[0, j : j + 1, :] * ext[j, 16:272, :]
            + taps[1, j : j + 1, :] * ext[j, 15:271, :]
            + taps[2, j : j + 1, :] * ext[j, 14:270, :]
        )
    sig[...] = gate[2] * gate[1]
    ss[...] = chunks(es, sig[...].astype(BF16))
    exchange(n, ss, sr, 0, ssem)
    await_all(n, hr, hsem.at[1])
    hf[...] = hr[...].astype(F32).reshape(520, 128)
    for c in range(4):
        hc[c] = hf[pl.ds(8 + c, 128, stride=4), :]
    build_toeplitz(hc, r_ref, 0, 1)

    cot_across.wait_recv()
    cot_forward = send(cotb.at[across], cotb.at[across], fsem.at[1], me, sibling)
    cot_sibling.wait_recv()
    cot_forward.wait_recv()
    load_out.wait()
    value = None
    for k in range(4):
        part = lax.dot_general(
            cotb[k],
            w_out[:, 256 * k : 256 * (k + 1)],
            (((1,), (1,)), ((), ())),
            preferred_element_type=F32,
        )
        value = part if value is None else value + part
    gg[...] = value
    gs[...] = value * gate[0]
    turned = jnp.dot(flip, gs[...].astype(BF16), preferred_element_type=F32).astype(BF16)
    gx[...] = chunks(es, turned)
    exchange(n, gx, gr, 0, gsem)

    build_toeplitz(hc, r_ref, 1, 4)
    await_all(n, sr, ssem.at[1])
    await_all(n, gr, gsem.at[1])
    shifted_blocks(sr, gr, sf, gf, xl)
    for pair in range(2):
        convolve(pair, xl, r_ref, yf, ys)
        exchange(n, ys.at[pair], yr.at[pair], 0, ysem.at[pair])
    back = None
    for pair in range(2):
        await_all(n, yr.at[pair], ysem.at[pair, 1])
        part = jnp.dot(cs[pair], yr[pair].reshape(512, 128), preferred_element_type=F32)
        back = part if back is None else back + part
    back = back.astype(BF16)
    state = jnp.concatenate([back[0:256], back[512:768]], axis=1)
    grad_signal = jnp.concatenate([back[256:512], back[768:1024]], axis=1)
    state = turn(eye, state) + skip[...] * sig[...]
    grad_signal = turn(flip, grad_signal) + skip[...] * gs[...]
    ups[0, 0:256, :] = gg[...] * state
    ups[1, 0:256, :] = grad_signal * gate[2]
    ups[2, 0:256, :] = grad_signal * gate[1]
    rim_copy = send(ups.at[:, pl.ds(0, 8)], edge, usem, earlier, p)

    def scatter_sum(which, product):
        half_send[which, 0] = product(sibling).astype(BF16)
        half_send[which, 1] = product(diagonal).astype(BF16)
        first = send(half_send.at[which], half_recv.at[which], rsem.at[which], me, sibling)
        own[which] = product(p)
        value = product(across)
        first.wait_recv()
        sum_send[which] = (value + half_recv[which, 1].astype(F32)).astype(BF16)
        second = send(sum_send.at[which], sum_recv.at[which], qsem.at[which], me, across)
        own[which] = own[which] + half_recv[which, 0].astype(F32)
        return first, second

    gated = (state * gate[0]).astype(BF16)

    def out_product(k):
        cols = pl.ds(pl.multiple_of(k * 256, 256), 256)
        return jnp.dot(gated, w_out[:, cols], preferred_element_type=F32)

    sent = scatter_sum(0, out_product)

    rim_copy.wait_recv()
    ups[:, 256:264, :] = edge[...] * (me < n - 1).astype(F32)
    for j in range(3):
        gp[j] = (
            taps[0, j : j + 1, :] * ups[j, 0:256, :]
            + taps[1, j : j + 1, :] * ups[j, 1:257, :]
            + taps[2, j : j + 1, :] * ups[j, 2:258, :]
        ).astype(BF16)

    def grad_product(k):
        rows = pl.ds(pl.multiple_of(k * 256, 256), 256)
        value = None
        for j in range(3):
            part = lax.dot_general(
                gp[j], w_in[j, rows, :], (((1,), (1,)), ((), ())), preferred_element_type=F32
            )
            value = part if value is None else value + part
        return value

    sent = sent + scatter_sum(1, grad_product)
    sent[1].wait_recv()
    out_ref[...] = (own[0] + sum_recv[0].astype(F32)).astype(BF16)
    sent[3].wait_recv()
    grad_ref[...] = (own[1] + sum_recv[1].astype(F32)).astype(BF16)

    for copy in (tok_across, tok_sibling, tok_forward, cot_across, cot_sibling, cot_forward, rim_copy):
        copy.wait_send()
    for copy in tuple(edges) + sent:
        copy.wait_send()
    await_all(n, hr, hsem.at[0])
    await_all(n, sr, ssem.at[0])
    await_all(n, gr, gsem.at[0])
    await_all(n, yr.at[0], ysem.at[0, 0])
    await_all(n, yr.at[1], ysem.at[1, 0])


def local(tokens, cotangent, in_weight, short_kernel, skip_gain, long_filter, out_weight):
    n = lax.axis_size("seq")
    out = jax.ShapeDtypeStruct((256, 256), BF16)
    vmem = pl.BlockSpec(memory_space=pltpu.VMEM)
    hbm = pl.BlockSpec(memory_space=pl.ANY)
    sem = pltpu.SemaphoreType.DMA
    return pl.pallas_call(
        functools.partial(block_kernel, n),
        out_shape=(out, out),
        in_specs=[vmem, vmem, hbm, vmem, vmem, vmem, hbm],
        out_specs=(vmem, vmem),
        scratch_shapes=[
            pltpu.VMEM((3, 1024, 256), BF16),
            pltpu.VMEM((256, 1024), BF16),
            pltpu.VMEM((4, 272, 256), BF16),
            pltpu.VMEM((4, 256, 256), BF16),
            pltpu.VMEM((3, 272, 256), F32),
            pltpu.VMEM((3, 256, 256), F32),
            pltpu.VMEM((256, 256), F32),
            pltpu.VMEM((256, 256), F32),
            pltpu.VMEM((256, 256), F32),
            pltpu.VMEM((2, 512, 256), BF16),
            pltpu.VMEM((2, 1024, 512), BF16),
            pltpu.VMEM((64, 8, 128), BF16),
            pltpu.VMEM((65, 8, 128), BF16),
            pltpu.VMEM((520, 128), F32),
            pltpu.VMEM((4, 128, 128), F32),
            pltpu.VMEM((64, 8, 128), BF16),
            pltpu.VMEM((64, 8, 128), BF16),
            pltpu.VMEM((512, 128), F32),
            pltpu.VMEM((64, 8, 128), BF16),
            pltpu.VMEM((64, 8, 128), BF16),
            pltpu.VMEM((512, 128), F32),
            pltpu.VMEM((4, 128, 2048), BF16),
            pltpu.VMEM((4, 256, 16384 + 128), BF16),
            pltpu.VMEM((512, 128), F32),
            pltpu.VMEM((2, 64, 8, 128), BF16),
            pltpu.VMEM((2, 64, 8, 128), BF16),
            pltpu.VMEM((3, 264, 256), F32),
            pltpu.VMEM((3, 8, 256), F32),
            pltpu.VMEM((3, 256, 256), BF16),
            pltpu.VMEM((2, 256, 256), F32),
            pltpu.VMEM((2, 2, 256, 256), BF16),
            pltpu.VMEM((2, 2, 256, 256), BF16),
            pltpu.VMEM((2, 256, 256), BF16),
            pltpu.VMEM((2, 256, 256), BF16),
            sem((2,)),
            sem((2, 2)),
            sem((2, 2)),
            sem((4, 2)),
            sem((2, 2)),
            sem((2,)),
            sem((2,)),
            sem((2,)),
            sem((2, 2)),
            sem((2,)),
            sem((2, 2)),
            sem((2, 2)),
        ],
        compiler_params=pltpu.CompilerParams(
            collective_id=0, has_side_effects=True, vmem_limit_bytes=58 * 2**20
        ),
    )(
        tokens,
        cotangent,
        in_weight,
        short_kernel,
        skip_gain.reshape(1, -1),
        long_filter,
        out_weight,
    )


def solution(mesh):
    placed = (
        P("seq", "panel"),
        P("seq", "panel"),
        P(None, None, "panel"),
        P(None, None, "panel"),
        P("panel"),
        P("seq", "panel"),
        P("panel", None),
    )
    return jax.shard_map(
        local,
        mesh=mesh,
        in_specs=placed,
        out_specs=(P("seq", "panel"), P("seq", "panel")),
        check_vma=False,
    )
```

```python
import functools

import jax
import jax.numpy as jnp
from jax import lax
from jax.experimental import pallas as pl
from jax.experimental.pallas import tpu as pltpu
from jax.sharding import PartitionSpec as P

F32, BF16 = jnp.float32, jnp.bfloat16


MESH = pl.DeviceIdType.MESH


def identity(flip):
    row = lax.broadcasted_iota(jnp.int32, (256, 256), 0)
    col = lax.broadcasted_iota(jnp.int32, (256, 256), 1)
    return jnp.where(row + col == 255 if flip else row == col, 1.0, 0.0).astype(BF16)


def turn(select, value):
    return lax.dot_general(select, value, (((1,), (1,)), ((), ())), preferred_element_type=F32)


def spread():
    half = lax.broadcasted_iota(jnp.int32, (2, 512, 256), 0)
    row = lax.broadcasted_iota(jnp.int32, (2, 512, 256), 1)
    col = lax.broadcasted_iota(jnp.int32, (2, 512, 256), 2)
    return jnp.where(col + (col // 4) * 4 + 4 * half == row, 1.0, 0.0).astype(BF16)


def collect(pair, cs):
    channel = lax.broadcasted_iota(jnp.int32, (256, 128), 0)
    source = (channel // 4) * 8 + channel % 2
    source = jnp.where((channel // 2) % 2 == pair, source, -1024)
    for tile in range(4):
        away = lax.broadcasted_iota(jnp.int32, (256, 128), 1) + 128 * tile - source
        for part in range(4):
            cs[pair, 256 * part : 256 * (part + 1), 128 * tile : 128 * (tile + 1)] = jnp.where(
                away == 2 * part, 1.0, 0.0
            ).astype(BF16)


def chunks(spread_ref, value):
    rows = turn(spread_ref[0], value[:128]) + turn(spread_ref[1], value[128:])
    return rows.reshape(64, 8, 128).astype(BF16)


def exchange(n, send_ref, recv_ref, offset, sems):
    me, p = lax.axis_index("seq"), lax.axis_index("panel")
    chip = p // 2
    across = (1 - chip) * 2 + lax.rem(p, 2)
    z, y, x = me // 16, lax.rem(me // 4, 4), lax.rem(me, 4)
    hops = {0: 0, 1: 1, 2: 2, 3: 1}
    steps = [(dz, dy, dx) for dz in (3, -3, 1, -1) for dy in range(4) for dx in range(4)]
    steps.sort(key=lambda s: -(abs(s[0]) + hops[s[1]] + hops[s[2]]))
    for dz, dy, dx in steps:
        to_z = lax.rem(z + (dz - 1) // 2 + chip + 4, 4)
        to = to_z * 16 + lax.rem(y + dy, 4) * 4 + lax.rem(x + dx, 4)
        pltpu.make_async_remote_copy(
            src_ref=send_ref.at[to],
            dst_ref=recv_ref.at[me + offset],
            send_sem=sems.at[0],
            recv_sem=sems.at[1],
            device_id={"seq": to, "panel": across},
            device_id_type=MESH,
        ).start()


def await_all(n, ref, sem):
    part = ref.at[pl.ds(0, n)]
    pltpu.make_async_copy(part, part, sem).wait()


def build_toeplitz(hc, r_ref, first, last):
    row = lax.broadcasted_iota(jnp.int32, (128, 128), 0)
    col = lax.broadcasted_iota(jnp.int32, (128, 128), 1)
    cut = col >= 128 - row

    def channel(c, carry):
        r_ref[c, 128:256, 0:128] = jnp.zeros((128, 128), BF16)
        early = jnp.zeros((128, 128), F32)
        for k in range(128):
            now = jnp.broadcast_to(hc[c, k : k + 1, :], (128, 128))
            mixed = jnp.where(cut, early, now)
            tile = pltpu.roll(mixed, 0, 1, stride=1, stride_axis=0).astype(BF16)
            at = 128 * k
            r_ref[c, 0:128, at : at + 128] = tile
            r_ref[c, 128:256, at + 128 : at + 256] = tile
            early = now
        return carry

    lax.fori_loop(first, last, channel, 0)


def shifted_blocks(sr, gr, sf, gf, xl):
    sf[...] = sr[...].astype(F32).reshape(512, 128)
    gf[...] = gr[...].astype(F32).reshape(512, 128)
    for c in range(4):
        rows = []
        for j in range(8):
            for ref, at in ((sf, 64 * j + c), (gf, 64 * (7 - j) + c)):
                rows.append(
                    jnp.concatenate(
                        [ref[pl.ds(at, 8, stride=8), :], ref[pl.ds(at + 4, 8, stride=8), :]], axis=1
                    )
                )
        x = jnp.concatenate(rows, axis=0).astype(BF16)
        xl[c, :, 0:256] = x
        for q in range(1, 8):
            xl[c, 0 : 16 * q, 256 * q : 256 * (q + 1)] = jnp.zeros((16 * q, 256), BF16)
            xl[c, 16 * q :, 256 * q : 256 * (q + 1)] = x[: 128 - 16 * q]


def convolve(pair, xl, r_ref, yf, ys):
    sub = lax.broadcasted_iota(jnp.int32, (8, 8, 256), 1)

    def channel(t, carry):
        c = 2 * pair + t
        total = [None, None]
        for r in range(8):
            z = None
            for q in range(8):
                at = (8 * q + r) * 256
                part = jnp.dot(
                    xl[c, :, 256 * q : 256 * (q + 1)],
                    r_ref[c, :, at : at + 256],
                    preferred_element_type=F32,
                )
                z = part if z is None else z + part
            z = z.reshape(8, 2, 8, 256)
            for side in range(2):
                zs = z[:, side]
                if r == 0:
                    total[side] = zs
                    continue
                turned = pltpu.roll(zs, r if side == 0 else 8 - r, 1)
                before = jnp.concatenate([jnp.zeros((1, 8, 256), F32), turned[:-1]], axis=0)
                inside = sub >= r if side == 0 else sub < 8 - r
                total[side] = total[side] + jnp.where(inside, turned, before)
        for side in range(2):
            for j in range(8):
                at = 64 * (j if side == 0 else 7 - j) + 2 * side
                yf[pl.ds(at + t, 8, stride=8), :] = total[side][j, :, 0:128]
                yf[pl.ds(at + 4 + t, 8, stride=8), :] = total[side][j, :, 128:256]
        return carry

    lax.fori_loop(0, 2, channel, 0)
    ys[pair] = yf[...].reshape(64, 8, 128).astype(BF16)


def block_kernel(
    n, tok, cot, w_in_hbm, taps, skip, filt, w_out_hbm, out_ref, grad_ref,
    w_in, w_out, tokb, cotb, ext, gate, sig, gg, gs, es, cs, hs, hr, hf, hc, ss, sr, sf, gx, gr, gf, xl, r_ref, yf, ys, yr,
    ups, edge, gp, own, other, half_send, half_recv, sum_send, sum_recv,
    wsem, tsem, fsem, esem, csem, hsem, ssem, gsem, ysem, usem, rsem, qsem,
):
    me, p = lax.axis_index("seq"), lax.axis_index("panel")
    core, chip = lax.rem(p, 2), p // 2
    sibling = chip * 2 + 1 - core
    across = (1 - chip) * 2 + core
    diagonal = (1 - chip) * 2 + 1 - core
    later, earlier = lax.rem(me + 1, n), lax.rem(me + n - 1, n)

    load_in = pltpu.make_async_copy(w_in_hbm, w_in, wsem.at[0])
    load_out = pltpu.make_async_copy(w_out_hbm, w_out, wsem.at[1])
    load_in.start()
    load_out.start()

    barrier = pltpu.get_barrier_semaphore()

    def signal(seq, panel):
        pl.semaphore_signal(
            barrier, inc=1, device_id={"seq": seq, "panel": panel}, device_id_type=MESH
        )

    signal(me, sibling)
    for peer in (p, sibling, diagonal):
        signal(earlier, peer)
    signal(later, p)

    def greet(j, carry):
        signal(lax.rem(me + j, n), across)
        return carry

    lax.fori_loop(0, n, greet, 0, unroll=8)

    def send(src, dst, sems, seq, panel):
        copy = pltpu.make_async_remote_copy(
            src_ref=src,
            dst_ref=dst,
            send_sem=sems.at[0],
            recv_sem=sems.at[1],
            device_id={"seq": seq, "panel": panel},
            device_id_type=MESH,
        )
        copy.start()
        return copy

    pl.semaphore_wait(barrier, n + 5)

    body = pl.ds(16, 256)
    rim = pl.ds(0, 16)
    edges = [
        send(tok.at[pl.ds(240, 16)], tokb.at[p, rim], esem.at[slot], later, panel)
        for slot, panel in enumerate((p, sibling, across, diagonal))
    ]
    tok_across = send(tok, tokb.at[p, body], tsem.at[0], me, across)
    tok_sibling = send(tok, tokb.at[p, body], tsem.at[1], me, sibling)
    es[...] = spread()
    hs[...] = chunks(es, filt[...].astype(BF16))
    hr[0] = jnp.zeros((8, 128), BF16)
    tokb[p, 16:272, :] = tok[...]
    cotb[p] = cot[...]
    tok_across.wait_send()
    cot_across = send(cot, cotb.at[p], csem.at[0], me, across)
    cot_sibling = send(cot, cotb.at[p], csem.at[1], me, sibling)
    collect(0, cs)
    collect(1, cs)
    eye, flip = identity(False), identity(True)
    tok_across.wait_recv()
    tok_forward = send(tokb.at[across, body], tokb.at[across, body], fsem.at[0], me, sibling)
    exchange(n, hs, hr, 1, hsem)
    tok_sibling.wait_recv()
    for copy in edges:
        copy.wait_recv()
    tok_forward.wait_recv()
    load_in.wait()

    started = (me > 0).astype(F32)
    for j in range(3):
        value = None
        for k in range(4):
            part = jnp.dot(
                tokb[k], w_in[j, 256 * k : 256 * (k + 1), :], preferred_element_type=F32
            )
            value = part if value is None else value + part
        value = value.astype(BF16).astype(F32)
        ext[j, 0:16, :] = value[0:16] * started
        ext[j, 16:272, :] = value[16:]
    for j in range(3):
        gate[j] = (
            taps[0, j : j + 1, :] * ext[j, 16:272, :]
            + taps[1, j : j + 1, :] * ext[j, 15:271, :]
            + taps[2, j : j + 1, :] * ext[j, 14:270, :]
        )
    sig[...] = gate[2] * gate[1]
    ss[...] = chunks(es, sig[...].astype(BF16))
    exchange(n, ss, sr, 0, ssem)
    cot_across.wait_recv()
    cot_forward = send(cotb.at[across], cotb.at[across], fsem.at[1], me, sibling)
    cot_sibling.wait_recv()
    cot_forward.wait_recv()
    load_out.wait()
    value = None
    for k in range(4):
        part = lax.dot_general(
            cotb[k],
            w_out[:, 256 * k : 256 * (k + 1)],
            (((1,), (1,)), ((), ())),
            preferred_element_type=F32,
        )
        value = part if value is None else value + part
    gg[...] = value
    gs[...] = value * gate[0]
    turned = jnp.dot(flip, gs[...].astype(BF16), preferred_element_type=F32).astype(BF16)
    gx[...] = chunks(es, turned)
    exchange(n, gx, gr, 0, gsem)

    await_all(n, hr, hsem.at[1])
    hf[...] = hr[...].astype(F32).reshape(520, 128)
    for c in range(4):
        hc[c] = hf[pl.ds(8 + c, 128, stride=4), :]
    build_toeplitz(hc, r_ref, 0, 4)
    await_all(n, sr, ssem.at[1])
    await_all(n, gr, gsem.at[1])
    shifted_blocks(sr, gr, sf, gf, xl)
    for pair in range(2):
        convolve(pair, xl, r_ref, yf, ys)
        exchange(n, ys.at[pair], yr.at[pair], 0, ysem.at[pair])
    back = None
    for pair in range(2):
        await_all(n, yr.at[pair], ysem.at[pair, 1])
        part = jnp.dot(cs[pair], yr[pair].reshape(512, 128), preferred_element_type=F32)
        back = part if back is None else back + part
    back = back.astype(BF16)
    state = jnp.concatenate([back[0:256], back[512:768]], axis=1)
    grad_signal = jnp.concatenate([back[256:512], back[768:1024]], axis=1)
    state = turn(eye, state) + skip[...] * sig[...]
    grad_signal = turn(flip, grad_signal) + skip[...] * gs[...]
    ups[0, 0:256, :] = gg[...] * state
    ups[1, 0:256, :] = grad_signal * gate[2]
    ups[2, 0:256, :] = grad_signal * gate[1]
    rim_copy = send(ups.at[:, pl.ds(0, 8)], edge, usem, earlier, p)

    def send_halves(which, product):
        half_send[which, 0] = product(sibling).astype(BF16)
        half_send[which, 1] = product(diagonal).astype(BF16)
        return send(half_send.at[which], half_recv.at[which], rsem.at[which], me, sibling)

    def send_sum(which, first):
        first.wait_recv()
        value = other[which] + half_recv[which, 1].astype(F32)
        sum_send[which] = value.astype(BF16)
        return send(sum_send.at[which], sum_recv.at[which], qsem.at[which], me, across)

    def finish(which, second):
        second.wait_recv()
        value = own[which] + half_recv[which, 0].astype(F32) + sum_recv[which].astype(F32)
        return value.astype(BF16)

    gated = (state * gate[0]).astype(BF16)

    def out_product(k):
        cols = pl.ds(pl.multiple_of(k * 256, 256), 256)
        return jnp.dot(gated, w_out[:, cols], preferred_element_type=F32)

    out_first = send_halves(0, out_product)
    other[0] = out_product(across)
    own[0] = out_product(p)

    rim_copy.wait_recv()
    ups[:, 256:264, :] = edge[...] * (me < n - 1).astype(F32)
    for j in range(3):
        gp[j] = (
            taps[0, j : j + 1, :] * ups[j, 0:256, :]
            + taps[1, j : j + 1, :] * ups[j, 1:257, :]
            + taps[2, j : j + 1, :] * ups[j, 2:258, :]
        ).astype(BF16)

    def grad_product(k):
        rows = pl.ds(pl.multiple_of(k * 256, 256), 256)
        value = None
        for j in range(3):
            part = lax.dot_general(
                gp[j], w_in[j, rows, :], (((1,), (1,)), ((), ())), preferred_element_type=F32
            )
            value = part if value is None else value + part
        return value

    grad_first = send_halves(1, grad_product)
    out_second = send_sum(0, out_first)
    other[1] = grad_product(across)
    grad_second = send_sum(1, grad_first)
    own[1] = grad_product(p)
    out_ref[...] = finish(0, out_second)
    grad_ref[...] = finish(1, grad_second)

    for copy in (tok_sibling, tok_forward, cot_across, cot_sibling, cot_forward, rim_copy):
        copy.wait_send()
    for copy in tuple(edges) + (out_first, out_second, grad_first, grad_second):
        copy.wait_send()
    await_all(n, hr, hsem.at[0])
    await_all(n, sr, ssem.at[0])
    await_all(n, gr, gsem.at[0])
    await_all(n, yr.at[0], ysem.at[0, 0])
    await_all(n, yr.at[1], ysem.at[1, 0])


def local(tokens, cotangent, in_weight, short_kernel, skip_gain, long_filter, out_weight):
    n = lax.axis_size("seq")
    out = jax.ShapeDtypeStruct((256, 256), BF16)
    vmem = pl.BlockSpec(memory_space=pltpu.VMEM)
    hbm = pl.BlockSpec(memory_space=pl.ANY)
    sem = pltpu.SemaphoreType.DMA
    return pl.pallas_call(
        functools.partial(block_kernel, n),
        out_shape=(out, out),
        in_specs=[vmem, vmem, hbm, vmem, vmem, vmem, hbm],
        out_specs=(vmem, vmem),
        scratch_shapes=[
            pltpu.VMEM((3, 1024, 256), BF16),
            pltpu.VMEM((256, 1024), BF16),
            pltpu.VMEM((4, 272, 256), BF16),
            pltpu.VMEM((4, 256, 256), BF16),
            pltpu.VMEM((3, 272, 256), F32),
            pltpu.VMEM((3, 256, 256), F32),
            pltpu.VMEM((256, 256), F32),
            pltpu.VMEM((256, 256), F32),
            pltpu.VMEM((256, 256), F32),
            pltpu.VMEM((2, 512, 256), BF16),
            pltpu.VMEM((2, 1024, 512), BF16),
            pltpu.VMEM((64, 8, 128), BF16),
            pltpu.VMEM((65, 8, 128), BF16),
            pltpu.VMEM((520, 128), F32),
            pltpu.VMEM((4, 128, 128), F32),
            pltpu.VMEM((64, 8, 128), BF16),
            pltpu.VMEM((64, 8, 128), BF16),
            pltpu.VMEM((512, 128), F32),
            pltpu.VMEM((64, 8, 128), BF16),
            pltpu.VMEM((64, 8, 128), BF16),
            pltpu.VMEM((512, 128), F32),
            pltpu.VMEM((4, 128, 2048), BF16),
            pltpu.VMEM((4, 256, 16384 + 128), BF16),
            pltpu.VMEM((512, 128), F32),
            pltpu.VMEM((2, 64, 8, 128), BF16),
            pltpu.VMEM((2, 64, 8, 128), BF16),
            pltpu.VMEM((3, 264, 256), F32),
            pltpu.VMEM((3, 8, 256), F32),
            pltpu.VMEM((3, 256, 256), BF16),
            pltpu.VMEM((2, 256, 256), F32),
            pltpu.VMEM((2, 256, 256), F32),
            pltpu.VMEM((2, 2, 256, 256), BF16),
            pltpu.VMEM((2, 2, 256, 256), BF16),
            pltpu.VMEM((2, 256, 256), BF16),
            pltpu.VMEM((2, 256, 256), BF16),
            sem((2,)),
            sem((2, 2)),
            sem((2, 2)),
            sem((4, 2)),
            sem((2, 2)),
            sem((2,)),
            sem((2,)),
            sem((2,)),
            sem((2, 2)),
            sem((2,)),
            sem((2, 2)),
            sem((2, 2)),
        ],
        compiler_params=pltpu.CompilerParams(
            collective_id=0, has_side_effects=True, vmem_limit_bytes=54 * 2**20
        ),
    )(
        tokens,
        cotangent,
        in_weight,
        short_kernel,
        skip_gain.reshape(1, -1),
        long_filter,
        out_weight,
    )


def solution(mesh):
    placed = (
        P("seq", "panel"),
        P("seq", "panel"),
        P(None, None, "panel"),
        P(None, None, "panel"),
        P("panel"),
        P("seq", "panel"),
        P("panel", None),
    )
    return jax.shard_map(
        local,
        mesh=mesh,
        in_specs=placed,
        out_specs=(P("seq", "panel"), P("seq", "panel")),
        check_vma=False,
    )
```

```python
import functools

import jax
import jax.numpy as jnp
from jax import lax
from jax.experimental import pallas as pl
from jax.experimental.pallas import tpu as pltpu
from jax.sharding import PartitionSpec as P

F32, BF16 = jnp.float32, jnp.bfloat16


MESH = pl.DeviceIdType.MESH


def identity(flip):
    row = lax.broadcasted_iota(jnp.int32, (256, 256), 0)
    col = lax.broadcasted_iota(jnp.int32, (256, 256), 1)
    return jnp.where(row + col == 255 if flip else row == col, 1.0, 0.0).astype(BF16)


def turn(select, value):
    return lax.dot_general(select, value, (((1,), (1,)), ((), ())), preferred_element_type=F32)


def spread():
    half = lax.broadcasted_iota(jnp.int32, (2, 512, 256), 0)
    row = lax.broadcasted_iota(jnp.int32, (2, 512, 256), 1)
    col = lax.broadcasted_iota(jnp.int32, (2, 512, 256), 2)
    return jnp.where(col + (col // 4) * 4 + 4 * half == row, 1.0, 0.0).astype(BF16)


def collect(pair, cs):
    channel = lax.broadcasted_iota(jnp.int32, (256, 128), 0)
    source = (channel // 4) * 8 + channel % 2
    source = jnp.where((channel // 2) % 2 == pair, source, -1024)
    for tile in range(4):
        away = lax.broadcasted_iota(jnp.int32, (256, 128), 1) + 128 * tile - source
        for part in range(4):
            cs[pair, 256 * part : 256 * (part + 1), 128 * tile : 128 * (tile + 1)] = jnp.where(
                away == 2 * part, 1.0, 0.0
            ).astype(BF16)


def chunks(spread_ref, value):
    rows = turn(spread_ref[0], value[:128]) + turn(spread_ref[1], value[128:])
    return rows.reshape(64, 8, 128).astype(BF16)


def exchange(n, send_ref, recv_ref, offset, sems):
    me, p = lax.axis_index("seq"), lax.axis_index("panel")
    chip = p // 2
    across = (1 - chip) * 2 + lax.rem(p, 2)
    z, y, x = me // 16, lax.rem(me // 4, 4), lax.rem(me, 4)
    hops = {0: 0, 1: 1, 2: 2, 3: 1}
    steps = [(dz, dy, dx) for dz in (3, -3, 1, -1) for dy in range(4) for dx in range(4)]
    steps.sort(key=lambda s: -(abs(s[0]) + hops[s[1]] + hops[s[2]]))
    for dz, dy, dx in steps:
        to_z = lax.rem(z + (dz - 1) // 2 + chip + 4, 4)
        to = to_z * 16 + lax.rem(y + dy, 4) * 4 + lax.rem(x + dx, 4)
        pltpu.make_async_remote_copy(
            src_ref=send_ref.at[to],
            dst_ref=recv_ref.at[me + offset],
            send_sem=sems.at[0],
            recv_sem=sems.at[1],
            device_id={"seq": to, "panel": across},
            device_id_type=MESH,
        ).start()


def await_all(n, ref, sem):
    part = ref.at[pl.ds(0, n)]
    pltpu.make_async_copy(part, part, sem).wait()


def build_toeplitz(hc, r_ref, first, last):
    row = lax.broadcasted_iota(jnp.int32, (128, 128), 0)
    col = lax.broadcasted_iota(jnp.int32, (128, 128), 1)
    cut = col >= 128 - row

    def channel(c, carry):
        r_ref[c, :, 0:128] = jnp.zeros((128, 128), BF16)
        early = jnp.zeros((128, 128), F32)
        for k in range(128):
            now = jnp.broadcast_to(hc[c, k : k + 1, :], (128, 128))
            mixed = jnp.where(cut, early, now)
            tile = pltpu.roll(mixed, 0, 1, stride=1, stride_axis=0).astype(BF16)
            r_ref[c, :, 128 * (k + 1) : 128 * (k + 2)] = tile
            early = now
        return carry

    lax.fori_loop(first, last, channel, 0)


def shifted_blocks(sr, gr, sf, gf, xl):
    sf[...] = sr[...].astype(F32).reshape(512, 128)
    gf[...] = gr[...].astype(F32).reshape(512, 128)
    for c in range(4):
        rows = []
        for j in range(8):
            for ref, at in ((sf, 64 * j + c), (gf, 64 * (7 - j) + c)):
                rows.append(
                    jnp.concatenate(
                        [ref[pl.ds(at, 8, stride=8), :], ref[pl.ds(at + 4, 8, stride=8), :]], axis=1
                    )
                )
        x = jnp.concatenate(rows, axis=0).astype(BF16)
        xl[c, :, 0:256] = x
        for q in range(1, 8):
            xl[c, 0 : 16 * q, 256 * q : 256 * (q + 1)] = jnp.zeros((16 * q, 256), BF16)
            xl[c, 16 * q :, 256 * q : 256 * (q + 1)] = x[: 128 - 16 * q]


def convolve(pair, xl, r_ref, yf, ys):
    sub = lax.broadcasted_iota(jnp.int32, (8, 8, 256), 1)

    def channel(t, carry):
        c = 2 * pair + t
        total = [None, None]
        for r in range(8):
            z = None
            for q in range(8):
                at = (8 * q + r) * 256
                lags = jnp.concatenate(
                    [r_ref[c, :, at + 128 : at + 384], r_ref[c, :, at : at + 256]], axis=0
                )
                part = jnp.dot(
                    xl[c, :, 256 * q : 256 * (q + 1)], lags, preferred_element_type=F32
                )
                z = part if z is None else z + part
            z = z.reshape(8, 2, 8, 256)
            for side in range(2):
                zs = z[:, side]
                if r == 0:
                    total[side] = zs
                    continue
                turned = pltpu.roll(zs, r if side == 0 else 8 - r, 1)
                before = jnp.concatenate([jnp.zeros((1, 8, 256), F32), turned[:-1]], axis=0)
                inside = sub >= r if side == 0 else sub < 8 - r
                total[side] = total[side] + jnp.where(inside, turned, before)
        for side in range(2):
            for j in range(8):
                at = 64 * (j if side == 0 else 7 - j) + 2 * side
                yf[pl.ds(at + t, 8, stride=8), :] = total[side][j, :, 0:128]
                yf[pl.ds(at + 4 + t, 8, stride=8), :] = total[side][j, :, 128:256]
        return carry

    lax.fori_loop(0, 2, channel, 0)
    ys[pair] = yf[...].reshape(64, 8, 128).astype(BF16)


def block_kernel(
    n, tok, cot, w_in_hbm, taps, skip, filt_hbm, w_out_hbm, out_ref,
    filt, w_in, w_out, tokb, cotb, ext, gate, sig, gg, gs, es, cs, hs, hr, hf, hc, ss, sr, sf, gx, gr, gf, xl, r_ref, yf, ys, yr,
    ups, head, edge, gp, own, other, half_send, half_recv, sum_send, sum_recv,
    wsem, tsem, fsem, esem, csem, hsem, ssem, gsem, ysem, usem, rsem, qsem,
):
    me, p = lax.axis_index("seq"), lax.axis_index("panel")
    core, chip = lax.rem(p, 2), p // 2
    sibling = chip * 2 + 1 - core
    across = (1 - chip) * 2 + core
    diagonal = (1 - chip) * 2 + 1 - core
    later, earlier = lax.rem(me + 1, n), lax.rem(me + n - 1, n)

    load_in = pltpu.make_async_copy(w_in_hbm, w_in, wsem.at[0])
    load_out = pltpu.make_async_copy(w_out_hbm, w_out, wsem.at[1])
    body = pl.ds(16, 256)
    rim = pl.ds(0, 16)
    load_filter = pltpu.make_async_copy(filt_hbm, filt, wsem.at[2])
    load_tok = pltpu.make_async_copy(tok, tokb.at[p, body], wsem.at[3])
    load_cot = pltpu.make_async_copy(cot, cotb.at[p], wsem.at[4])
    for load in (load_filter, load_tok, load_cot, load_in, load_out):
        load.start()

    barrier = pltpu.get_barrier_semaphore()

    def signal(seq, panel):
        pl.semaphore_signal(
            barrier, inc=1, device_id={"seq": seq, "panel": panel}, device_id_type=MESH
        )

    signal(me, sibling)
    for peer in (p, sibling, diagonal):
        signal(earlier, peer)
    signal(later, p)

    def greet(j, carry):
        signal(lax.rem(me + j, n), across)
        return carry

    lax.fori_loop(0, n, greet, 0, unroll=8)

    def send(src, dst, sems, seq, panel):
        copy = pltpu.make_async_remote_copy(
            src_ref=src,
            dst_ref=dst,
            send_sem=sems.at[0],
            recv_sem=sems.at[1],
            device_id={"seq": seq, "panel": panel},
            device_id_type=MESH,
        )
        copy.start()
        return copy

    pl.semaphore_wait(barrier, n + 5)

    edges = [
        send(tok.at[pl.ds(240, 16)], tokb.at[p, rim], esem.at[slot], later, panel)
        for slot, panel in enumerate((p, sibling, across, diagonal))
    ]
    tok_across = send(tok, tokb.at[p, body], tsem.at[0], me, across)
    tok_sibling = send(tok, tokb.at[p, body], tsem.at[1], me, sibling)
    es[...] = spread()
    load_filter.wait()
    hs[...] = chunks(es, filt[...].astype(BF16))
    hr[0] = jnp.zeros((8, 128), BF16)
    tok_across.wait_send()
    cot_across = send(cot, cotb.at[p], csem.at[0], me, across)
    cot_sibling = send(cot, cotb.at[p], csem.at[1], me, sibling)
    collect(0, cs)
    collect(1, cs)
    eye, flip = identity(False), identity(True)
    tok_across.wait_recv()
    tok_forward = send(tokb.at[across, body], tokb.at[across, body], fsem.at[0], me, sibling)
    exchange(n, hs, hr, 1, hsem)
    tok_sibling.wait_recv()
    for copy in edges:
        copy.wait_recv()
    tok_forward.wait_recv()
    load_in.wait()
    load_tok.wait()

    started = (me > 0).astype(F32)
    for j in range(3):
        value = None
        for k in range(4):
            part = jnp.dot(
                tokb[k], w_in[j, 256 * k : 256 * (k + 1), :], preferred_element_type=F32
            )
            value = part if value is None else value + part
        value = value.astype(BF16).astype(F32)
        ext[j, 0:16, :] = value[0:16] * started
        ext[j, 16:272, :] = value[16:]
    for j in range(3):
        gate[j] = (
            taps[0, j : j + 1, :] * ext[j, 16:272, :]
            + taps[1, j : j + 1, :] * ext[j, 15:271, :]
            + taps[2, j : j + 1, :] * ext[j, 14:270, :]
        )
    sig[...] = gate[2] * gate[1]
    ss[...] = chunks(es, sig[...].astype(BF16))
    exchange(n, ss, sr, 0, ssem)
    cot_across.wait_recv()
    cot_forward = send(cotb.at[across], cotb.at[across], fsem.at[1], me, sibling)
    cot_sibling.wait_recv()
    cot_forward.wait_recv()
    load_out.wait()
    load_cot.wait()
    value = None
    for k in range(4):
        part = lax.dot_general(
            cotb[k],
            w_out[:, 256 * k : 256 * (k + 1)],
            (((1,), (1,)), ((), ())),
            preferred_element_type=F32,
        )
        value = part if value is None else value + part
    gg[...] = value
    gs[...] = value * gate[0]
    turned = jnp.dot(flip, gs[...].astype(BF16), preferred_element_type=F32).astype(BF16)
    gx[...] = chunks(es, turned)
    exchange(n, gx, gr, 0, gsem)

    await_all(n, hr, hsem.at[1])
    hf[...] = hr[...].astype(F32).reshape(520, 128)
    for c in range(4):
        hc[c] = hf[pl.ds(8 + c, 128, stride=4), :]
    build_toeplitz(hc, r_ref, 0, 4)
    await_all(n, sr, ssem.at[1])
    await_all(n, gr, gsem.at[1])
    shifted_blocks(sr, gr, sf, gf, xl)
    for pair in range(2):
        convolve(pair, xl, r_ref, yf, ys)
        exchange(n, ys.at[pair], yr.at[pair], 0, ysem.at[pair])
    back = None
    for pair in range(2):
        await_all(n, yr.at[pair], ysem.at[pair, 1])
        part = jnp.dot(cs[pair], yr[pair].reshape(512, 128), preferred_element_type=F32)
        back = part if back is None else back + part
    back = back.astype(BF16)
    state = jnp.concatenate([back[0:256], back[512:768]], axis=1)
    grad_signal = jnp.concatenate([back[256:512], back[768:1024]], axis=1)
    head_state = turn(eye[0:8], state) + skip[...] * sig[0:8, :]
    head_grad = turn(flip[0:8], grad_signal) + skip[...] * gs[0:8, :]
    head[0] = gg[0:8, :] * head_state
    head[1] = head_grad * gate[2, 0:8, :]
    head[2] = head_grad * gate[1, 0:8, :]
    rim_copy = send(head, edge, usem, earlier, p)
    state = turn(eye, state) + skip[...] * sig[...]
    grad_signal = turn(flip, grad_signal) + skip[...] * gs[...]

    def send_halves(which, product):
        half_send[which, 0] = product(sibling).astype(BF16)
        half_send[which, 1] = product(diagonal).astype(BF16)
        return send(half_send.at[which], half_recv.at[which], rsem.at[which], me, sibling)

    def send_sum(which, first):
        first.wait_recv()
        value = other[which] + half_recv[which, 1].astype(F32)
        sum_send[which] = value.astype(BF16)
        return send(sum_send.at[which], sum_recv.at[which], qsem.at[which], me, across)

    def finish(which, second):
        second.wait_recv()
        value = own[which] + half_recv[which, 0].astype(F32) + sum_recv[which].astype(F32)
        return value.astype(BF16)

    gated = (state * gate[0]).astype(BF16)

    def out_product(k):
        cols = pl.ds(pl.multiple_of(k * 256, 256), 256)
        return jnp.dot(gated, w_out[:, cols], preferred_element_type=F32)

    out_first = send_halves(0, out_product)
    other[0] = out_product(across)
    ups[0, 0:256, :] = gg[...] * state
    ups[1, 0:256, :] = grad_signal * gate[2]
    ups[2, 0:256, :] = grad_signal * gate[1]
    own[0] = out_product(p)
    out_second = send_sum(0, out_first)

    rim_copy.wait_recv()
    ups[:, 256:264, :] = edge[...] * (me < n - 1).astype(F32)
    for j in range(3):
        gp[j] = (
            taps[0, j : j + 1, :] * ups[j, 0:256, :]
            + taps[1, j : j + 1, :] * ups[j, 1:257, :]
            + taps[2, j : j + 1, :] * ups[j, 2:258, :]
        ).astype(BF16)

    def grad_product(k):
        rows = pl.ds(pl.multiple_of(k * 256, 256), 256)
        value = None
        for j in range(3):
            part = lax.dot_general(
                gp[j], w_in[j, rows, :], (((1,), (1,)), ((), ())), preferred_element_type=F32
            )
            value = part if value is None else value + part
        return value

    grad_first = send_halves(1, grad_product)
    other[1] = grad_product(across)
    grad_second = send_sum(1, grad_first)
    own[1] = grad_product(p)
    out_ref[0] = finish(0, out_second)
    out_ref[1] = finish(1, grad_second)

    for copy in (tok_sibling, tok_forward, cot_across, cot_sibling, cot_forward, rim_copy):
        copy.wait_send()
    for copy in tuple(edges) + (out_first, out_second, grad_first, grad_second):
        copy.wait_send()
    await_all(n, hr, hsem.at[0])
    await_all(n, sr, ssem.at[0])
    await_all(n, gr, gsem.at[0])
    await_all(n, yr.at[0], ysem.at[0, 0])
    await_all(n, yr.at[1], ysem.at[1, 0])


def local(tokens, cotangent, in_weight, short_kernel, skip_gain, long_filter, out_weight):
    n = lax.axis_size("seq")
    vmem = pl.BlockSpec(memory_space=pltpu.VMEM)
    hbm = pl.BlockSpec(memory_space=pltpu.HBM)
    sem = pltpu.SemaphoreType.DMA
    both = pl.pallas_call(
        functools.partial(block_kernel, n),
        out_shape=jax.ShapeDtypeStruct((2, 256, 256), BF16),
        in_specs=[hbm, hbm, hbm, vmem, vmem, hbm, hbm],
        out_specs=vmem,
        scratch_shapes=[
            pltpu.VMEM((256, 256), F32),
            pltpu.VMEM((3, 1024, 256), BF16),
            pltpu.VMEM((256, 1024), BF16),
            pltpu.VMEM((4, 272, 256), BF16),
            pltpu.VMEM((4, 256, 256), BF16),
            pltpu.VMEM((3, 272, 256), F32),
            pltpu.VMEM((3, 256, 256), F32),
            pltpu.VMEM((256, 256), F32),
            pltpu.VMEM((256, 256), F32),
            pltpu.VMEM((256, 256), F32),
            pltpu.VMEM((2, 512, 256), BF16),
            pltpu.VMEM((2, 1024, 512), BF16),
            pltpu.VMEM((64, 8, 128), BF16),
            pltpu.VMEM((65, 8, 128), BF16),
            pltpu.VMEM((520, 128), F32),
            pltpu.VMEM((4, 128, 128), F32),
            pltpu.VMEM((64, 8, 128), BF16),
            pltpu.VMEM((64, 8, 128), BF16),
            pltpu.VMEM((512, 128), F32),
            pltpu.VMEM((64, 8, 128), BF16),
            pltpu.VMEM((64, 8, 128), BF16),
            pltpu.VMEM((512, 128), F32),
            pltpu.VMEM((4, 128, 2048), BF16),
            pltpu.VMEM((4, 128, 16384 + 128), BF16),
            pltpu.VMEM((512, 128), F32),
            pltpu.VMEM((2, 64, 8, 128), BF16),
            pltpu.VMEM((2, 64, 8, 128), BF16),
            pltpu.VMEM((3, 264, 256), F32),
            pltpu.VMEM((3, 8, 256), F32),
            pltpu.VMEM((3, 8, 256), F32),
            pltpu.VMEM((3, 256, 256), BF16),
            pltpu.VMEM((2, 256, 256), F32),
            pltpu.VMEM((2, 256, 256), F32),
            pltpu.VMEM((2, 2, 256, 256), BF16),
            pltpu.VMEM((2, 2, 256, 256), BF16),
            pltpu.VMEM((2, 256, 256), BF16),
            pltpu.VMEM((2, 256, 256), BF16),
            sem((5,)),
            sem((2, 2)),
            sem((2, 2)),
            sem((4, 2)),
            sem((2, 2)),
            sem((2,)),
            sem((2,)),
            sem((2,)),
            sem((2, 2)),
            sem((2,)),
            sem((2, 2)),
            sem((2, 2)),
        ],
        compiler_params=pltpu.CompilerParams(
            collective_id=0, has_side_effects=True, vmem_limit_bytes=55 * 2**20
        ),
    )(
        tokens,
        cotangent,
        in_weight,
        short_kernel,
        skip_gain.reshape(1, -1),
        long_filter,
        out_weight,
    )
    return both[0], both[1]


def solution(mesh):
    placed = (
        P("seq", "panel"),
        P("seq", "panel"),
        P(None, None, "panel"),
        P(None, None, "panel"),
        P("panel"),
        P("seq", "panel"),
        P("panel", None),
    )
    return jax.shard_map(
        local,
        mesh=mesh,
        in_specs=placed,
        out_specs=(P("seq", "panel"), P("seq", "panel")),
        check_vma=False,
    )
```

```python
import functools

import jax
import jax.numpy as jnp
from jax import lax
from jax.experimental import pallas as pl
from jax.experimental.pallas import tpu as pltpu
from jax.sharding import PartitionSpec as P

F32, BF16 = jnp.float32, jnp.bfloat16


MESH = pl.DeviceIdType.MESH


def identity(flip):
    row = lax.broadcasted_iota(jnp.int32, (256, 256), 0)
    col = lax.broadcasted_iota(jnp.int32, (256, 256), 1)
    return jnp.where(row + col == 255 if flip else row == col, 1.0, 0.0).astype(BF16)


def turn(select, value):
    return lax.dot_general(select, value, (((1,), (1,)), ((), ())), preferred_element_type=F32)


def spread():
    half = lax.broadcasted_iota(jnp.int32, (2, 512, 256), 0)
    row = lax.broadcasted_iota(jnp.int32, (2, 512, 256), 1)
    col = lax.broadcasted_iota(jnp.int32, (2, 512, 256), 2)
    return jnp.where(col + (col // 4) * 4 + 4 * half == row, 1.0, 0.0).astype(BF16)


def collect(pair, cs):
    channel = lax.broadcasted_iota(jnp.int32, (256, 128), 0)
    source = (channel // 4) * 8 + channel % 2
    source = jnp.where((channel // 2) % 2 == pair, source, -1024)
    for tile in range(4):
        away = lax.broadcasted_iota(jnp.int32, (256, 128), 1) + 128 * tile - source
        for part in range(4):
            cs[pair, 256 * part : 256 * (part + 1), 128 * tile : 128 * (tile + 1)] = jnp.where(
                away == 2 * part, 1.0, 0.0
            ).astype(BF16)


def chunks(spread_ref, value):
    rows = turn(spread_ref[0], value[:128]) + turn(spread_ref[1], value[128:])
    return rows.reshape(64, 8, 128).astype(BF16)


def exchange(n, send_ref, recv_ref, offset, sems):
    me, p = lax.axis_index("seq"), lax.axis_index("panel")
    chip = p // 2
    across = (1 - chip) * 2 + lax.rem(p, 2)
    z, y, x = me // 16, lax.rem(me // 4, 4), lax.rem(me, 4)
    hops = {0: 0, 1: 1, 2: 2, 3: 1}
    steps = [(dz, dy, dx) for dz in (3, -3, 1, -1) for dy in range(4) for dx in range(4)]
    steps.sort(key=lambda s: -(abs(s[0]) + hops[s[1]] + hops[s[2]]))
    for dz, dy, dx in steps:
        to_z = lax.rem(z + (dz - 1) // 2 + chip + 4, 4)
        to = to_z * 16 + lax.rem(y + dy, 4) * 4 + lax.rem(x + dx, 4)
        pltpu.make_async_remote_copy(
            src_ref=send_ref.at[to],
            dst_ref=recv_ref.at[me + offset],
            send_sem=sems.at[0],
            recv_sem=sems.at[1],
            device_id={"seq": to, "panel": across},
            device_id_type=MESH,
        ).start()


def await_all(n, ref, sem):
    part = ref.at[pl.ds(0, n)]
    pltpu.make_async_copy(part, part, sem).wait()


def build_toeplitz(hc, r_ref, first, last):
    row = lax.broadcasted_iota(jnp.int32, (128, 128), 0)
    col = lax.broadcasted_iota(jnp.int32, (128, 128), 1)
    cut = col >= 128 - row

    def channel(c, carry):
        r_ref[c, :, 0:128] = jnp.zeros((128, 128), BF16)
        early = jnp.zeros((128, 128), F32)
        for k in range(128):
            now = jnp.broadcast_to(hc[c, k : k + 1, :], (128, 128))
            mixed = jnp.where(cut, early, now)
            tile = pltpu.roll(mixed, 0, 1, stride=1, stride_axis=0).astype(BF16)
            r_ref[c, :, 128 * (k + 1) : 128 * (k + 2)] = tile
            early = now
        return carry

    lax.fori_loop(first, last, channel, 0)


def shifted_blocks(sr, gr, sf, gf, xl):
    sf[...] = sr[...].astype(F32).reshape(512, 128)
    gf[...] = gr[...].astype(F32).reshape(512, 128)
    for c in range(4):
        rows = []
        for j in range(8):
            for ref, at in ((sf, 64 * j + c), (gf, 64 * (7 - j) + c)):
                rows.append(
                    jnp.concatenate(
                        [ref[pl.ds(at, 8, stride=8), :], ref[pl.ds(at + 4, 8, stride=8), :]], axis=1
                    )
                )
        x = jnp.concatenate(rows, axis=0).astype(BF16)
        xl[c, :, 0:256] = x
        for q in range(1, 8):
            xl[c, 0 : 16 * q, 256 * q : 256 * (q + 1)] = jnp.zeros((16 * q, 256), BF16)
            xl[c, 16 * q :, 256 * q : 256 * (q + 1)] = x[: 128 - 16 * q]


def convolve(pair, xl, r_ref, yf, ys):
    sub = lax.broadcasted_iota(jnp.int32, (8, 8, 256), 1)

    def channel(t, carry):
        c = 2 * pair + t
        total = [None, None]
        for r in range(8):
            z = None
            for q in range(8):
                at = (8 * q + r) * 256
                lags = jnp.concatenate(
                    [r_ref[c, :, at + 128 : at + 384], r_ref[c, :, at : at + 256]], axis=0
                )
                part = jnp.dot(
                    xl[c, :, 256 * q : 256 * (q + 1)], lags, preferred_element_type=F32
                )
                z = part if z is None else z + part
            z = z.reshape(8, 2, 8, 256)
            for side in range(2):
                zs = z[:, side]
                if r == 0:
                    total[side] = zs
                    continue
                turned = pltpu.roll(zs, r if side == 0 else 8 - r, 1)
                before = jnp.concatenate([jnp.zeros((1, 8, 256), F32), turned[:-1]], axis=0)
                inside = sub >= r if side == 0 else sub < 8 - r
                total[side] = total[side] + jnp.where(inside, turned, before)
        for side in range(2):
            for j in range(8):
                at = 64 * (j if side == 0 else 7 - j) + 2 * side
                yf[pl.ds(at + t, 8, stride=8), :] = total[side][j, :, 0:128]
                yf[pl.ds(at + 4 + t, 8, stride=8), :] = total[side][j, :, 128:256]
        return carry

    lax.fori_loop(0, 2, channel, 0)
    ys[pair] = yf[...].reshape(64, 8, 128).astype(BF16)


def block_kernel(
    n, tok, cot, w_in_hbm, taps, skip, filt_hbm, w_out_hbm, out_ref,
    filt, w_in, w_out, tokb, cotb, ext, gate, sig, gg, gs, es, cs, hs, hr, hf, hc, ss, sr, sf, gx, gr, gf, xl, r_ref, yf, ys, yr,
    ups, head, edge, gp, own, other, half_send, half_recv, sum_send, sum_recv,
    wsem, tsem, fsem, esem, csem, hsem, ssem, gsem, ysem, usem, rsem, qsem,
):
    me, p = lax.axis_index("seq"), lax.axis_index("panel")
    core, chip = lax.rem(p, 2), p // 2
    sibling = chip * 2 + 1 - core
    across = (1 - chip) * 2 + core
    diagonal = (1 - chip) * 2 + 1 - core
    later, earlier = lax.rem(me + 1, n), lax.rem(me + n - 1, n)

    load_in = pltpu.make_async_copy(w_in_hbm, w_in, wsem.at[0])
    load_out = pltpu.make_async_copy(w_out_hbm, w_out, wsem.at[1])
    body = pl.ds(16, 256)
    rim = pl.ds(0, 16)
    load_filter = pltpu.make_async_copy(filt_hbm, filt, wsem.at[2])
    load_tok = pltpu.make_async_copy(tok, tokb.at[p, body], wsem.at[3])
    load_cot = pltpu.make_async_copy(cot, cotb.at[p], wsem.at[4])
    for load in (load_filter, load_tok, load_cot, load_in, load_out):
        load.start()

    barrier = pltpu.get_barrier_semaphore()

    def signal(seq, panel):
        pl.semaphore_signal(
            barrier, inc=1, device_id={"seq": seq, "panel": panel}, device_id_type=MESH
        )

    signal(me, sibling)
    for peer in (p, sibling, diagonal):
        signal(earlier, peer)
    signal(later, p)

    def greet(j, carry):
        signal(lax.rem(me + j, n), across)
        return carry

    lax.fori_loop(0, n, greet, 0, unroll=8)

    def send(src, dst, sems, seq, panel):
        copy = pltpu.make_async_remote_copy(
            src_ref=src,
            dst_ref=dst,
            send_sem=sems.at[0],
            recv_sem=sems.at[1],
            device_id={"seq": seq, "panel": panel},
            device_id_type=MESH,
        )
        copy.start()
        return copy

    pl.semaphore_wait(barrier, n + 5)

    edges = [
        send(tok.at[pl.ds(240, 16)], tokb.at[p, rim], esem.at[slot], later, panel)
        for slot, panel in enumerate((p, sibling, across, diagonal))
    ]
    tok_across = send(tok, tokb.at[p, body], tsem.at[0], me, across)
    tok_sibling = send(tok, tokb.at[p, body], tsem.at[1], me, sibling)
    es[...] = spread()
    load_filter.wait()
    hs[...] = chunks(es, filt[...].astype(BF16))
    hr[0] = jnp.zeros((8, 128), BF16)
    tok_across.wait_send()
    cot_across = send(cot, cotb.at[p], csem.at[0], me, across)
    cot_sibling = send(cot, cotb.at[p], csem.at[1], me, sibling)
    collect(0, cs)
    collect(1, cs)
    eye, flip = identity(False), identity(True)
    tok_across.wait_recv()
    tok_forward = send(tokb.at[across, body], tokb.at[across, body], fsem.at[0], me, sibling)
    exchange(n, hs, hr, 1, hsem)
    tok_sibling.wait_recv()
    for copy in edges:
        copy.wait_recv()
    tok_forward.wait_recv()
    load_in.wait()
    load_tok.wait()

    started = (me > 0).astype(F32)
    for j in range(3):
        value = None
        for k in range(4):
            part = jnp.dot(
                tokb[k], w_in[j, 256 * k : 256 * (k + 1), :], preferred_element_type=F32
            )
            value = part if value is None else value + part
        value = value.astype(BF16).astype(F32)
        ext[j, 0:16, :] = value[0:16] * started
        ext[j, 16:272, :] = value[16:]
    for j in range(3):
        gate[j] = (
            taps[0, j : j + 1, :] * ext[j, 16:272, :]
            + taps[1, j : j + 1, :] * ext[j, 15:271, :]
            + taps[2, j : j + 1, :] * ext[j, 14:270, :]
        )
    sig[...] = gate[2] * gate[1]
    ss[...] = chunks(es, sig[...].astype(BF16))
    exchange(n, ss, sr, 0, ssem)
    cot_across.wait_recv()
    cot_forward = send(cotb.at[across], cotb.at[across], fsem.at[1], me, sibling)
    cot_sibling.wait_recv()
    cot_forward.wait_recv()
    load_out.wait()
    load_cot.wait()
    value = None
    for k in range(4):
        part = lax.dot_general(
            cotb[k],
            w_out[:, 256 * k : 256 * (k + 1)],
            (((1,), (1,)), ((), ())),
            preferred_element_type=F32,
        )
        value = part if value is None else value + part
    gg[...] = value
    gs[...] = value * gate[0]
    turned = jnp.dot(flip, gs[...].astype(BF16), preferred_element_type=F32).astype(BF16)
    gx[...] = chunks(es, turned)
    exchange(n, gx, gr, 0, gsem)

    await_all(n, hr, hsem.at[1])
    hf[...] = hr[...].astype(F32).reshape(520, 128)
    for c in range(4):
        hc[c] = hf[pl.ds(8 + c, 128, stride=4), :]
    build_toeplitz(hc, r_ref, 0, 4)
    await_all(n, sr, ssem.at[1])
    await_all(n, gr, gsem.at[1])
    shifted_blocks(sr, gr, sf, gf, xl)
    for pair in range(2):
        convolve(pair, xl, r_ref, yf, ys)
        exchange(n, ys.at[pair], yr.at[pair], 0, ysem.at[pair])
    back = None
    for pair in range(2):
        await_all(n, yr.at[pair], ysem.at[pair, 1])
        part = jnp.dot(cs[pair], yr[pair].reshape(512, 128), preferred_element_type=F32)
        back = part if back is None else back + part
    back = back.astype(BF16)
    state = jnp.concatenate([back[0:256], back[512:768]], axis=1)
    grad_signal = jnp.concatenate([back[256:512], back[768:1024]], axis=1)
    head_state = turn(eye[0:8], state) + skip[...] * sig[0:8, :]
    head_grad = turn(flip[0:8], grad_signal) + skip[...] * gs[0:8, :]
    head[0] = gg[0:8, :] * head_state
    head[1] = head_grad * gate[2, 0:8, :]
    head[2] = head_grad * gate[1, 0:8, :]
    rim_copy = send(head, edge, usem, earlier, p)
    state = turn(eye, state) + skip[...] * sig[...]
    grad_signal = turn(flip, grad_signal) + skip[...] * gs[...]

    def send_halves(which, product):
        half_send[which, 0] = product(sibling).astype(BF16)
        half_send[which, 1] = product(diagonal).astype(BF16)
        return send(half_send.at[which], half_recv.at[which], rsem.at[which], me, sibling)

    def send_sum(which, first):
        first.wait_recv()
        value = other[which] + half_recv[which, 1].astype(F32)
        sum_send[which] = value.astype(BF16)
        return send(sum_send.at[which], sum_recv.at[which], qsem.at[which], me, across)

    def finish(which, second):
        second.wait_recv()
        value = own[which] + half_recv[which, 0].astype(F32) + sum_recv[which].astype(F32)
        return value.astype(BF16)

    gated = (state * gate[0]).astype(BF16)

    def out_product(k):
        cols = pl.ds(pl.multiple_of(k * 256, 256), 256)
        return jnp.dot(gated, w_out[:, cols], preferred_element_type=F32)

    out_first = send_halves(0, out_product)
    other[0] = out_product(across)
    ups[0, 0:256, :] = gg[...] * state
    ups[1, 0:256, :] = grad_signal * gate[2]
    ups[2, 0:256, :] = grad_signal * gate[1]
    own[0] = out_product(p)
    out_second = send_sum(0, out_first)

    rim_copy.wait_recv()
    ups[:, 256:264, :] = edge[...] * (me < n - 1).astype(F32)
    for j in range(3):
        gp[j] = (
            taps[0, j : j + 1, :] * ups[j, 0:256, :]
            + taps[1, j : j + 1, :] * ups[j, 1:257, :]
            + taps[2, j : j + 1, :] * ups[j, 2:258, :]
        ).astype(BF16)

    def grad_product(k):
        rows = pl.ds(pl.multiple_of(k * 256, 256), 256)
        value = None
        for j in range(3):
            part = lax.dot_general(
                gp[j], w_in[j, rows, :], (((1,), (1,)), ((), ())), preferred_element_type=F32
            )
            value = part if value is None else value + part
        return value

    grad_first = send_halves(1, grad_product)
    other[1] = grad_product(across)
    grad_second = send_sum(1, grad_first)
    own[1] = grad_product(p)
    out_ref[0] = finish(0, out_second)
    out_ref[1] = finish(1, grad_second)

    for copy in (tok_sibling, tok_forward, cot_across, cot_sibling, cot_forward, rim_copy):
        copy.wait_send()
    for copy in tuple(edges) + (out_first, out_second, grad_first, grad_second):
        copy.wait_send()
    await_all(n, hr, hsem.at[0])
    await_all(n, sr, ssem.at[0])
    await_all(n, gr, gsem.at[0])
    await_all(n, yr.at[0], ysem.at[0, 0])
    await_all(n, yr.at[1], ysem.at[1, 0])


def local(tokens, cotangent, in_weight, short_kernel, skip_gain, long_filter, out_weight):
    n = lax.axis_size("seq")
    vmem = pl.BlockSpec(memory_space=pltpu.VMEM)
    hbm = pl.BlockSpec(memory_space=pltpu.HBM)
    sem = pltpu.SemaphoreType.DMA
    both = pl.pallas_call(
        functools.partial(block_kernel, n),
        out_shape=pltpu.VMEM((2, 256, 256), BF16),
        in_specs=[hbm, hbm, hbm, vmem, vmem, hbm, hbm],
        out_specs=vmem,
        scratch_shapes=[
            pltpu.VMEM((256, 256), F32),
            pltpu.VMEM((3, 1024, 256), BF16),
            pltpu.VMEM((256, 1024), BF16),
            pltpu.VMEM((4, 272, 256), BF16),
            pltpu.VMEM((4, 256, 256), BF16),
            pltpu.VMEM((3, 272, 256), F32),
            pltpu.VMEM((3, 256, 256), F32),
            pltpu.VMEM((256, 256), F32),
            pltpu.VMEM((256, 256), F32),
            pltpu.VMEM((256, 256), F32),
            pltpu.VMEM((2, 512, 256), BF16),
            pltpu.VMEM((2, 1024, 512), BF16),
            pltpu.VMEM((64, 8, 128), BF16),
            pltpu.VMEM((65, 8, 128), BF16),
            pltpu.VMEM((520, 128), F32),
            pltpu.VMEM((4, 128, 128), F32),
            pltpu.VMEM((64, 8, 128), BF16),
            pltpu.VMEM((64, 8, 128), BF16),
            pltpu.VMEM((512, 128), F32),
            pltpu.VMEM((64, 8, 128), BF16),
            pltpu.VMEM((64, 8, 128), BF16),
            pltpu.VMEM((512, 128), F32),
            pltpu.VMEM((4, 128, 2048), BF16),
            pltpu.VMEM((4, 128, 16384 + 128), BF16),
            pltpu.VMEM((512, 128), F32),
            pltpu.VMEM((2, 64, 8, 128), BF16),
            pltpu.VMEM((2, 64, 8, 128), BF16),
            pltpu.VMEM((3, 264, 256), F32),
            pltpu.VMEM((3, 8, 256), F32),
            pltpu.VMEM((3, 8, 256), F32),
            pltpu.VMEM((3, 256, 256), BF16),
            pltpu.VMEM((2, 256, 256), F32),
            pltpu.VMEM((2, 256, 256), F32),
            pltpu.VMEM((2, 2, 256, 256), BF16),
            pltpu.VMEM((2, 2, 256, 256), BF16),
            pltpu.VMEM((2, 256, 256), BF16),
            pltpu.VMEM((2, 256, 256), BF16),
            sem((5,)),
            sem((2, 2)),
            sem((2, 2)),
            sem((4, 2)),
            sem((2, 2)),
            sem((2,)),
            sem((2,)),
            sem((2,)),
            sem((2, 2)),
            sem((2,)),
            sem((2, 2)),
            sem((2, 2)),
        ],
        compiler_params=pltpu.CompilerParams(
            collective_id=0, has_side_effects=True, vmem_limit_bytes=55 * 2**20
        ),
    )(
        tokens,
        cotangent,
        in_weight,
        short_kernel,
        skip_gain.reshape(1, -1),
        long_filter,
        out_weight,
    )
    return both[0], both[1]


def solution(mesh):
    placed = (
        P("seq", "panel"),
        P("seq", "panel"),
        P(None, None, "panel"),
        P(None, None, "panel"),
        P("panel"),
        P("seq", "panel"),
        P("panel", None),
    )
    return jax.shard_map(
        local,
        mesh=mesh,
        in_specs=placed,
        out_specs=(P("seq", "panel"), P("seq", "panel")),
        check_vma=False,
    )
```

```python
import functools

import jax
import jax.numpy as jnp
from jax import lax
from jax.experimental import pallas as pl
from jax.experimental.pallas import tpu as pltpu
from jax.sharding import PartitionSpec as P

F32, BF16 = jnp.float32, jnp.bfloat16


MESH = pl.DeviceIdType.MESH


def identity(flip):
    row = lax.broadcasted_iota(jnp.int32, (256, 256), 0)
    col = lax.broadcasted_iota(jnp.int32, (256, 256), 1)
    return jnp.where(row + col == 255 if flip else row == col, 1.0, 0.0).astype(BF16)


def turn(select, value):
    return lax.dot_general(select, value, (((1,), (1,)), ((), ())), preferred_element_type=F32)


def spread():
    half = lax.broadcasted_iota(jnp.int32, (2, 512, 256), 0)
    row = lax.broadcasted_iota(jnp.int32, (2, 512, 256), 1)
    col = lax.broadcasted_iota(jnp.int32, (2, 512, 256), 2)
    return jnp.where(col + (col // 4) * 4 + 4 * half == row, 1.0, 0.0).astype(BF16)


def collect(pair, cs):
    channel = lax.broadcasted_iota(jnp.int32, (256, 128), 0)
    source = (channel // 4) * 8 + channel % 2
    source = jnp.where((channel // 2) % 2 == pair, source, -1024)
    for tile in range(4):
        away = lax.broadcasted_iota(jnp.int32, (256, 128), 1) + 128 * tile - source
        for part in range(4):
            cs[pair, 256 * part : 256 * (part + 1), 128 * tile : 128 * (tile + 1)] = jnp.where(
                away == 2 * part, 1.0, 0.0
            ).astype(BF16)


def chunks(spread_ref, value):
    rows = turn(spread_ref[0], value[:128]) + turn(spread_ref[1], value[128:])
    return rows.reshape(64, 8, 128).astype(BF16)


def exchange(n, send_ref, recv_ref, offset, sems):
    me, p = lax.axis_index("seq"), lax.axis_index("panel")
    chip = p // 2
    across = (1 - chip) * 2 + lax.rem(p, 2)
    z, y, x = me // 16, lax.rem(me // 4, 4), lax.rem(me, 4)
    hops = {0: 0, 1: 1, 2: 2, 3: 1}
    steps = [(dz, dy, dx) for dz in (3, -3, 1, -1) for dy in range(4) for dx in range(4)]
    steps.sort(key=lambda s: -(abs(s[0]) + hops[s[1]] + hops[s[2]]))
    for dz, dy, dx in steps:
        to_z = lax.rem(z + (dz - 1) // 2 + chip + 4, 4)
        to = to_z * 16 + lax.rem(y + dy, 4) * 4 + lax.rem(x + dx, 4)
        pltpu.make_async_remote_copy(
            src_ref=send_ref.at[to],
            dst_ref=recv_ref.at[me + offset],
            send_sem=sems.at[0],
            recv_sem=sems.at[1],
            device_id={"seq": to, "panel": across},
            device_id_type=MESH,
        ).start()


def await_all(n, ref, sem):
    part = ref.at[pl.ds(0, n)]
    pltpu.make_async_copy(part, part, sem).wait()


def build_toeplitz(hc, r_ref, first, last):
    row = lax.broadcasted_iota(jnp.int32, (128, 128), 0)
    col = lax.broadcasted_iota(jnp.int32, (128, 128), 1)
    cut = col >= 128 - row

    def channel(c, carry):
        r_ref[c, :, 0:128] = jnp.zeros((128, 128), BF16)
        early = jnp.zeros((128, 128), F32)
        for k in range(128):
            now = jnp.broadcast_to(hc[c, k : k + 1, :], (128, 128))
            mixed = jnp.where(cut, early, now)
            tile = pltpu.roll(mixed, 0, 1, stride=1, stride_axis=0).astype(BF16)
            r_ref[c, :, 128 * (k + 1) : 128 * (k + 2)] = tile
            early = now
        return carry

    lax.fori_loop(first, last, channel, 0)


def shifted_blocks(sr, gr, sf, gf, xl):
    sf[...] = sr[...].astype(F32).reshape(512, 128)
    gf[...] = gr[...].astype(F32).reshape(512, 128)
    for c in range(4):
        rows = []
        for j in range(8):
            for ref, at in ((sf, 64 * j + c), (gf, 64 * (7 - j) + c)):
                rows.append(
                    jnp.concatenate(
                        [ref[pl.ds(at, 8, stride=8), :], ref[pl.ds(at + 4, 8, stride=8), :]], axis=1
                    )
                )
        x = jnp.concatenate(rows, axis=0).astype(BF16)
        xl[c, :, 0:256] = x
        for q in range(1, 8):
            xl[c, 16 * q :, 256 * q : 256 * (q + 1)] = x[: 128 - 16 * q]


def convolve(pair, xl, r_ref, yf, ys):
    sub = lax.broadcasted_iota(jnp.int32, (8, 8, 256), 1)

    def channel(t, carry):
        c = 2 * pair + t
        total = [None, None]
        for r in range(8):
            z = None
            for q in range(8):
                at = (8 * q + r) * 256
                lags = jnp.concatenate(
                    [r_ref[c, :, at + 128 : at + 384], r_ref[c, :, at : at + 256]], axis=0
                )
                part = jnp.dot(
                    xl[c, :, 256 * q : 256 * (q + 1)], lags, preferred_element_type=F32
                )
                z = part if z is None else z + part
            z = z.reshape(8, 2, 8, 256)
            for side in range(2):
                zs = z[:, side]
                if r == 0:
                    total[side] = zs
                    continue
                turned = pltpu.roll(zs, r if side == 0 else 8 - r, 1)
                before = jnp.concatenate([jnp.zeros((1, 8, 256), F32), turned[:-1]], axis=0)
                inside = sub >= r if side == 0 else sub < 8 - r
                total[side] = total[side] + jnp.where(inside, turned, before)
        for side in range(2):
            for j in range(8):
                at = 64 * (j if side == 0 else 7 - j) + 2 * side
                yf[pl.ds(at + t, 8, stride=8), :] = total[side][j, :, 0:128]
                yf[pl.ds(at + 4 + t, 8, stride=8), :] = total[side][j, :, 128:256]
        return carry

    lax.fori_loop(0, 2, channel, 0)
    ys[pair] = yf[...].reshape(64, 8, 128).astype(BF16)


def block_kernel(
    n, tok, cot, w_in_hbm, taps, skip, filt_hbm, w_out_hbm, out_ref,
    filt, w_in, w_out, tokb, cotb, ext, gate, sig, gg, gs, es, cs, hs, hr, hf, hc, ss, sr, sf, gx, gr, gf, xl, r_ref, yf, ys, yr,
    ups, head, edge, gp, own, other, half_send, half_recv, sum_send, sum_recv,
    wsem, tsem, fsem, esem, csem, hsem, ssem, gsem, ysem, usem, rsem, qsem,
):
    me, p = lax.axis_index("seq"), lax.axis_index("panel")
    core, chip = lax.rem(p, 2), p // 2
    sibling = chip * 2 + 1 - core
    across = (1 - chip) * 2 + core
    diagonal = (1 - chip) * 2 + 1 - core
    later, earlier = lax.rem(me + 1, n), lax.rem(me + n - 1, n)

    load_in = pltpu.make_async_copy(w_in_hbm, w_in, wsem.at[0])
    load_out = pltpu.make_async_copy(w_out_hbm, w_out, wsem.at[1])
    body = pl.ds(16, 256)
    rim = pl.ds(0, 16)
    load_filter = pltpu.make_async_copy(filt_hbm, filt, wsem.at[2])
    load_tok = pltpu.make_async_copy(tok, tokb.at[p, body], wsem.at[3])
    load_cot = pltpu.make_async_copy(cot, cotb.at[p], wsem.at[4])
    for load in (load_filter, load_tok, load_cot, load_in, load_out):
        load.start()

    barrier = pltpu.get_barrier_semaphore()

    def signal(seq, panel):
        pl.semaphore_signal(
            barrier, inc=1, device_id={"seq": seq, "panel": panel}, device_id_type=MESH
        )

    signal(me, sibling)
    for peer in (p, sibling, diagonal):
        signal(earlier, peer)
    signal(later, p)

    def greet(j, carry):
        signal(lax.rem(me + j, n), across)
        return carry

    lax.fori_loop(0, n, greet, 0, unroll=8)

    def send(src, dst, sems, seq, panel):
        copy = pltpu.make_async_remote_copy(
            src_ref=src,
            dst_ref=dst,
            send_sem=sems.at[0],
            recv_sem=sems.at[1],
            device_id={"seq": seq, "panel": panel},
            device_id_type=MESH,
        )
        copy.start()
        return copy

    pl.semaphore_wait(barrier, n + 5)

    edges = [
        send(tok.at[pl.ds(240, 16)], tokb.at[p, rim], esem.at[slot], later, panel)
        for slot, panel in enumerate((p, sibling, across, diagonal))
    ]
    tok_across = send(tok, tokb.at[p, body], tsem.at[0], me, across)
    tok_sibling = send(tok, tokb.at[p, body], tsem.at[1], me, sibling)
    cot_across = send(cot, cotb.at[p], csem.at[0], me, across)
    cot_sibling = send(cot, cotb.at[p], csem.at[1], me, sibling)
    es[...] = spread()
    load_filter.wait()
    hs[...] = chunks(es, filt[...].astype(BF16))
    hr[0] = jnp.zeros((8, 128), BF16)
    collect(0, cs)
    collect(1, cs)
    eye, flip = identity(False), identity(True)
    tok_across.wait_recv()
    tok_forward = send(tokb.at[across, body], tokb.at[across, body], fsem.at[0], me, sibling)
    exchange(n, hs, hr, 1, hsem)
    tok_sibling.wait_recv()
    for copy in edges:
        copy.wait_recv()
    tok_forward.wait_recv()
    load_in.wait()
    load_tok.wait()

    started = (me > 0).astype(F32)
    def branch(j):
        value = None
        for k in range(4):
            part = jnp.dot(
                tokb[k], w_in[j, 256 * k : 256 * (k + 1), :], preferred_element_type=F32
            )
            value = part if value is None else value + part
        value = value.astype(BF16).astype(F32)
        ext[j, 0:16, :] = value[0:16] * started
        ext[j, 16:272, :] = value[16:]
        gate[j] = (
            taps[0, j : j + 1, :] * ext[j, 16:272, :]
            + taps[1, j : j + 1, :] * ext[j, 15:271, :]
            + taps[2, j : j + 1, :] * ext[j, 14:270, :]
        )

    branch(1)
    branch(2)
    sig[...] = gate[2] * gate[1]
    ss[...] = chunks(es, sig[...].astype(BF16))
    exchange(n, ss, sr, 0, ssem)
    branch(0)
    cot_across.wait_recv()
    cot_forward = send(cotb.at[across], cotb.at[across], fsem.at[1], me, sibling)
    cot_sibling.wait_recv()
    cot_forward.wait_recv()
    load_out.wait()
    load_cot.wait()
    value = None
    for k in range(4):
        part = lax.dot_general(
            cotb[k],
            w_out[:, 256 * k : 256 * (k + 1)],
            (((1,), (1,)), ((), ())),
            preferred_element_type=F32,
        )
        value = part if value is None else value + part
    gg[...] = value
    gs[...] = value * gate[0]
    turned = jnp.dot(flip, gs[...].astype(BF16), preferred_element_type=F32).astype(BF16)
    gx[...] = chunks(es, turned)
    exchange(n, gx, gr, 0, gsem)

    await_all(n, hr, hsem.at[1])
    hf[...] = hr[...].astype(F32).reshape(520, 128)
    for c in range(4):
        hc[c] = hf[pl.ds(8 + c, 128, stride=4), :]
    build_toeplitz(hc, r_ref, 0, 4)
    for c in range(4):
        for q in range(1, 8):
            xl[c, 0 : 16 * q, 256 * q : 256 * (q + 1)] = jnp.zeros((16 * q, 256), BF16)
    await_all(n, sr, ssem.at[1])
    await_all(n, gr, gsem.at[1])
    shifted_blocks(sr, gr, sf, gf, xl)
    for pair in range(2):
        convolve(pair, xl, r_ref, yf, ys)
        exchange(n, ys.at[pair], yr.at[pair], 0, ysem.at[pair])
    back = None
    for pair in range(2):
        await_all(n, yr.at[pair], ysem.at[pair, 1])
        part = jnp.dot(cs[pair], yr[pair].reshape(512, 128), preferred_element_type=F32)
        back = part if back is None else back + part
    back = back.astype(BF16)
    state = jnp.concatenate([back[0:256], back[512:768]], axis=1)
    grad_signal = jnp.concatenate([back[256:512], back[768:1024]], axis=1)
    head_state = turn(eye[0:8], state) + skip[...] * sig[0:8, :]
    head_grad = turn(flip[0:8], grad_signal) + skip[...] * gs[0:8, :]
    head[0] = gg[0:8, :] * head_state
    head[1] = head_grad * gate[2, 0:8, :]
    head[2] = head_grad * gate[1, 0:8, :]
    rim_copy = send(head, edge, usem, earlier, p)
    state = turn(eye, state) + skip[...] * sig[...]
    grad_signal = turn(flip, grad_signal) + skip[...] * gs[...]

    def send_halves(which, product):
        half_send[which, 0] = product(sibling).astype(BF16)
        half_send[which, 1] = product(diagonal).astype(BF16)
        return send(half_send.at[which], half_recv.at[which], rsem.at[which], me, sibling)

    def send_sum(which, first):
        first.wait_recv()
        value = other[which] + half_recv[which, 1].astype(F32)
        sum_send[which] = value.astype(BF16)
        return send(sum_send.at[which], sum_recv.at[which], qsem.at[which], me, across)

    def finish(which, second):
        second.wait_recv()
        value = own[which] + half_recv[which, 0].astype(F32) + sum_recv[which].astype(F32)
        return value.astype(BF16)

    gated = (state * gate[0]).astype(BF16)

    def out_product(k):
        cols = pl.ds(pl.multiple_of(k * 256, 256), 256)
        return jnp.dot(gated, w_out[:, cols], preferred_element_type=F32)

    out_first = send_halves(0, out_product)
    other[0] = out_product(across)
    ups[0, 0:256, :] = gg[...] * state
    ups[1, 0:256, :] = grad_signal * gate[2]
    ups[2, 0:256, :] = grad_signal * gate[1]
    own[0] = out_product(p)
    out_second = send_sum(0, out_first)

    rim_copy.wait_recv()
    ups[:, 256:264, :] = edge[...] * (me < n - 1).astype(F32)
    for j in range(3):
        gp[j] = (
            taps[0, j : j + 1, :] * ups[j, 0:256, :]
            + taps[1, j : j + 1, :] * ups[j, 1:257, :]
            + taps[2, j : j + 1, :] * ups[j, 2:258, :]
        ).astype(BF16)

    def grad_product(k):
        rows = pl.ds(pl.multiple_of(k * 256, 256), 256)
        value = None
        for j in range(3):
            part = lax.dot_general(
                gp[j], w_in[j, rows, :], (((1,), (1,)), ((), ())), preferred_element_type=F32
            )
            value = part if value is None else value + part
        return value

    grad_first = send_halves(1, grad_product)
    other[1] = grad_product(across)
    grad_second = send_sum(1, grad_first)
    own[1] = grad_product(p)
    out_ref[0] = finish(0, out_second)
    out_ref[1] = finish(1, grad_second)

    for copy in (tok_across, tok_sibling, tok_forward, cot_across, cot_sibling, cot_forward, rim_copy):
        copy.wait_send()
    for copy in tuple(edges) + (out_first, out_second, grad_first, grad_second):
        copy.wait_send()
    await_all(n, hr, hsem.at[0])
    await_all(n, sr, ssem.at[0])
    await_all(n, gr, gsem.at[0])
    await_all(n, yr.at[0], ysem.at[0, 0])
    await_all(n, yr.at[1], ysem.at[1, 0])


def local(tokens, cotangent, in_weight, short_kernel, skip_gain, long_filter, out_weight):
    n = lax.axis_size("seq")
    vmem = pl.BlockSpec(memory_space=pltpu.VMEM)
    hbm = pl.BlockSpec(memory_space=pltpu.HBM)
    sem = pltpu.SemaphoreType.DMA
    both = pl.pallas_call(
        functools.partial(block_kernel, n),
        out_shape=pltpu.VMEM((2, 256, 256), BF16),
        in_specs=[hbm, hbm, hbm, vmem, vmem, hbm, hbm],
        out_specs=vmem,
        scratch_shapes=[
            pltpu.VMEM((256, 256), F32),
            pltpu.VMEM((3, 1024, 256), BF16),
            pltpu.VMEM((256, 1024), BF16),
            pltpu.VMEM((4, 272, 256), BF16),
            pltpu.VMEM((4, 256, 256), BF16),
            pltpu.VMEM((3, 272, 256), F32),
            pltpu.VMEM((3, 256, 256), F32),
            pltpu.VMEM((256, 256), F32),
            pltpu.VMEM((256, 256), F32),
            pltpu.VMEM((256, 256), F32),
            pltpu.VMEM((2, 512, 256), BF16),
            pltpu.VMEM((2, 1024, 512), BF16),
            pltpu.VMEM((64, 8, 128), BF16),
            pltpu.VMEM((65, 8, 128), BF16),
            pltpu.VMEM((520, 128), F32),
            pltpu.VMEM((4, 128, 128), F32),
            pltpu.VMEM((64, 8, 128), BF16),
            pltpu.VMEM((64, 8, 128), BF16),
            pltpu.VMEM((512, 128), F32),
            pltpu.VMEM((64, 8, 128), BF16),
            pltpu.VMEM((64, 8, 128), BF16),
            pltpu.VMEM((512, 128), F32),
            pltpu.VMEM((4, 128, 2048), BF16),
            pltpu.VMEM((4, 128, 16384 + 128), BF16),
            pltpu.VMEM((512, 128), F32),
            pltpu.VMEM((2, 64, 8, 128), BF16),
            pltpu.VMEM((2, 64, 8, 128), BF16),
            pltpu.VMEM((3, 264, 256), F32),
            pltpu.VMEM((3, 8, 256), F32),
            pltpu.VMEM((3, 8, 256), F32),
            pltpu.VMEM((3, 256, 256), BF16),
            pltpu.VMEM((2, 256, 256), F32),
            pltpu.VMEM((2, 256, 256), F32),
            pltpu.VMEM((2, 2, 256, 256), BF16),
            pltpu.VMEM((2, 2, 256, 256), BF16),
            pltpu.VMEM((2, 256, 256), BF16),
            pltpu.VMEM((2, 256, 256), BF16),
            sem((5,)),
            sem((2, 2)),
            sem((2, 2)),
            sem((4, 2)),
            sem((2, 2)),
            sem((2,)),
            sem((2,)),
            sem((2,)),
            sem((2, 2)),
            sem((2,)),
            sem((2, 2)),
            sem((2, 2)),
        ],
        compiler_params=pltpu.CompilerParams(
            collective_id=0, has_side_effects=True, vmem_limit_bytes=55 * 2**20
        ),
    )(
        tokens,
        cotangent,
        in_weight,
        short_kernel,
        skip_gain.reshape(1, -1),
        long_filter,
        out_weight,
    )
    return both[0], both[1]


def solution(mesh):
    placed = (
        P("seq", "panel"),
        P("seq", "panel"),
        P(None, None, "panel"),
        P(None, None, "panel"),
        P("panel"),
        P("seq", "panel"),
        P("panel", None),
    )
    return jax.shard_map(
        local,
        mesh=mesh,
        in_specs=placed,
        out_specs=(P("seq", "panel"), P("seq", "panel")),
        check_vma=False,
    )
```
